32 devices in a mesh: wide: 8 (over z, x), narrow: 4 (over y, core).
Axes of the slice: x: 2, y: 2, z: 4, core: 2. Of those that a mesh axis runs over, the one named last changes fastest.
Arguments:
- tokens: bfloat16 [64, 512, 512], P(('wide', 'narrow')), may hold values from -6 to 6
- segment_ids: int32 [64, 512], P(('wide', 'narrow')), may hold values from 0 to 3, never falling along the last dimension, each value on 1 to 256 neighbouring positions
- matrices: bfloat16 [2, 5120, 512], P(None, ('wide', 'narrow')), may hold values from -1.5 to 1.5, as said below
- vectors: bfloat16 [2, 2560], replicated, may hold values from 0.5 to 1.5
- cotangent: bfloat16 [64, 512, 512], P(('wide', 'narrow')), may hold values from -6 to 6
Outputs:
- outputs: float32 [64, 512, 512], P(('wide', 'narrow'))
- input_grad: float32 [64, 512, 512], P(('wide', 'narrow'))
- matrix_grads: float32 [2, 5120, 512], P(None, ('wide', 'narrow'))
- vector_grads: float32 [2, 2560], replicated
The draws below stay inside these ranges and needn't reach their ends.
Inputs may be any that keep to these rules, and one draw needn't show every extreme that they name: `segment_ids`: in each row the document numbers start at 0 and never fall; no document is longer than half of 512 positions. `matrices`: matrix entries are symmetric about zero.
All inputs are finite; a program needn't handle non-finite values.
Results may differ from the reference program's by a relative error of at most 0.0095.
Values may be sent and summed in bfloat16 or wider, within the bound.
A program may use at most 256 MiB of HBM per device.

```python
import math
import jax
import jax.numpy as jnp
import numpy as np
from jax import lax

D = 512
FF = 3072
S = 512
LAYERS = 2
SEGS = 4
ROWS = 64
VEC = 2560


def draw_matrices(key, part):
    key = jax.random.fold_in(key, 7)
    half_width = FF // 2
    counts = (FF, half_width, S)
    scales = (D ** (-0.5), half_width ** (-0.5), (S // 4) ** (-0.5))
    stacked = []
    for layer_index in range(LAYERS):
        sub_keys = jax.random.split(jax.random.fold_in(key, layer_index), 3)
        pieces = []
        for piece_index in range(3):
            shape = (counts[piece_index], D)
            unit = jax.random.truncated_normal(sub_keys[piece_index], -3.0, 3.0, shape, jnp.float32)
            pieces.append(unit * scales[piece_index])
        stacked.append(jnp.concatenate(pieces, axis=0))
    return jnp.stack(stacked).astype(jnp.bfloat16)


def level_of(stream_key, extent, cuts, smallest, top_value):
    factor_of, own = 1.0, jax.random.fold_in(stream_key, 6)
    for axis_at, blocks in cuts:
        steps = jnp.exp(jax.random.uniform(jax.random.fold_in(own, axis_at), (blocks,), jnp.float32, smallest / len(cuts), top_value / len(cuts)))
        factor_of = factor_of * jnp.repeat(steps, extent[axis_at] // blocks).reshape([-1 if axis == axis_at else 1 for axis in range(len(extent))])
    return factor_of


def profile(count, total, most, skew):
    portions = [(1 << 20) // math.isqrt(grade ** skew) + 1 for grade in range(2, count + 1)]
    spare, holding = total - most - (count - 1), [1] * (count - 1)
    while spare > 0:
        movable = [i for i in range(count - 1) if holding[i] < most]
        pool, budget = sum([portions[i] for i in movable]), spare
        for i in movable:
            more = min(most - holding[i], max(1, budget * portions[i] // pool), spare)
            holding[i] = holding[i] + more
            spare = spare - more
    return np.array([most] + holding)


def ragged(key, count, total, reach, skew):
    if count == 2:
        one = jax.random.randint(key, (), max(1, total - reach), min(reach, total - 1) + 1)
        return jnp.stack([one, total - one])
    lengths = jnp.asarray(profile(count, total, reach, skew), jnp.int32)
    couples = (count - 1) // 2
    donor, taker = lengths[1:1 + 2 * couples:2], lengths[2:2 + 2 * couples:2]
    slack = jnp.minimum(donor - 1, reach - taker)
    moved = jax.random.randint(jax.random.fold_in(key, 1), (couples,), 0, 1 << 20) % (slack + 1)
    lengths = lengths.at[1:1 + 2 * couples:2].set(donor - moved).at[2:2 + 2 * couples:2].set(taker + moved)
    return lengths[jax.random.permutation(jax.random.fold_in(key, 2), count)]


def centred(own_key, extent, scale, bound, cuts=(), held_as=jnp.bfloat16):
    level = level_of(own_key, extent, cuts, -0.22, 0.18) if cuts else 1.0
    values = jax.random.normal(own_key, extent, jnp.float32) * scale * level
    return jnp.minimum(jnp.maximum(values, -bound), bound).astype(held_as)


def setup_inputs(seed: int = 0) -> dict:
    arg_keys = jax.random.split(jax.random.key(seed), 6)
    tokens = centred(arg_keys[0], (ROWS, S, D), 1.0, 6.0, ((0, 32),))
    segment_ids = jax.vmap(lambda own: jnp.searchsorted(jnp.cumsum(ragged(own, SEGS, S, S // 2, 2)), jnp.arange(S), side="right"))(jax.random.split(arg_keys[1], ROWS)).reshape((ROWS, S)).astype(jnp.int32)
    matrices = draw_matrices(jax.random.fold_in(arg_keys[5], 71), 0)
    vectors = jnp.clip(jax.random.uniform(arg_keys[3], (LAYERS, VEC), jnp.float32, 0.5, 1.5), 0.5, 1.5).astype(jnp.bfloat16)
    cotangent = centred(arg_keys[4], (ROWS, S, D), 1.0, 6.0, ((0, 32),))
    return {"tokens": tokens, "segment_ids": segment_ids, "matrices": matrices, "vectors": vectors, "cotangent": cotangent}


@jax.custom_vjp
def low(v):
    return lax.optimization_barrier(v.astype(jnp.bfloat16)).astype(jnp.float32)

@jax.custom_vjp
def low_back(v):
    return v

def low_keep(v):
    return (low(v), None)

def low_pass(kept, grad):
    return (grad,)

def back_keep(v):
    return (v, None)

def back_low(kept, grad):
    return (low(grad),)
low.defvjp(low_keep, low_pass)
low_back.defvjp(back_keep, back_low)
EPSILON = 1e-05
HIGHEST = lax.Precision.HIGHEST

def layer_norm(values, gain):
    center = values - lax.optimization_barrier(jnp.mean(values, axis=-1, keepdims=True))
    spread = lax.optimization_barrier(jnp.mean(center * center, axis=-1, keepdims=True))
    return center * lax.rsqrt(spread + EPSILON) * gain

def block(inputs, mats, vecs, mask):
    half_width = FF // 2
    w_in_t = mats[:FF]
    w_out = mats[FF:FF + half_width]
    w_spatial = mats[FF + half_width:]
    gain_in = vecs[:D]
    gain_mid = vecs[D:D + half_width]
    bias_spatial = vecs[D + half_width:]
    normed = low(layer_norm(inputs, gain_in))
    hidden_pre = low_back(jnp.einsum('gsd,fd->gsf', normed, w_in_t, precision=HIGHEST))
    hidden = jax.nn.gelu(hidden_pre)
    spatial_in = low(layer_norm(hidden[..., half_width:], gain_mid))
    mixed = low_back(jnp.einsum('gij,gjc->gic', w_spatial[None] * mask, spatial_in, precision=HIGHEST) + bias_spatial[None, :, None])
    product = low(hidden[..., :half_width] * mixed)
    branch = low_back(jnp.einsum('gsc,cd->gsd', product, w_out, precision=HIGHEST))
    return inputs + branch

def reference(tokens, segment_ids, matrices, vectors, cotangent):
    mats_all = matrices.astype(jnp.float32)
    vecs_all = vectors.astype(jnp.float32)
    group = math.gcd(ROWS, max(1, 4096 // S))
    count = ROWS // group
    inputs_all = tokens.astype(jnp.float32).reshape(count, group, S, D)
    segs_all = segment_ids.reshape(count, group, S)
    cots_all = cotangent.astype(jnp.float32).reshape(count, group, S, D)

    def step(totals, item):
        inputs, segs, cots = item
        mask = (segs[:, :, None] == segs[:, None, :]).astype(jnp.float32)

        def forward(values, mats, vecs):
            for layer_index in range(LAYERS):
                values = block(values, mats[layer_index], vecs[layer_index], mask)
            return values
        result, pull = jax.vjp(forward, inputs, mats_all, vecs_all)
        grad_inputs, grad_mats, grad_vecs = pull(cots)
        return ((totals[0] + grad_mats, totals[1] + grad_vecs), (result, grad_inputs))
    totals, (results, grad_all) = lax.scan(step, (jnp.zeros_like(mats_all), jnp.zeros_like(vecs_all)), (inputs_all, segs_all, cots_all))
    return (results.reshape(ROWS, S, D), grad_all.reshape(ROWS, S, D), totals[0], totals[1])
```

```python
import functools

import jax
import jax.numpy as jnp
from jax import lax
from jax.experimental import pallas as pl
from jax.experimental.pallas import tpu as pltpu
from jax.sharding import PartitionSpec as P

D = 512
FF = 3072
HALF = FF // 2
S = 512
LAYERS = 2
VEC = D + HALF + S
ALL_ROWS = FF + HALF + S
EPSILON = 1e-05
BLOCK = 512
MESH = pl.DeviceIdType.MESH
BF16 = jnp.bfloat16
F32 = jnp.float32
GELU_A = 0.7978845608028654
GELU_B = 0.044715


def dot(left, right, left_dim, right_dim):
    dims = (((left_dim,), (right_dim,)), ((), ()))
    return lax.dot_general(left, right, dims, preferred_element_type=F32)


def gelu_and_slope(z):
    squared = z * z
    tanh = jnp.tanh(z * (GELU_A + (GELU_A * GELU_B) * squared))
    half_z = 0.5 * z
    value = half_z + half_z * tanh
    slope = (0.5 + 0.5 * tanh) + (half_z * (1.0 - tanh * tanh)) * (
        GELU_A + (3.0 * GELU_A * GELU_B) * squared
    )
    return value, slope


def lane_groups(values):
    total = values[:, :128]
    for at in range(128, values.shape[1], 128):
        total = total + values[:, at : at + 128]
    return total


def lanes(column, width):
    return jnp.concatenate([column] * (width // 128), axis=1)


class Links:
    def __init__(self, wide, narrow, share):
        self.share = share
        self.levels = wide // 2
        self.narrow = narrow
        self.w = lax.axis_index("wide")
        self.n = lax.axis_index("narrow")
        self.x = self.w % 2
        self.z = self.w // 2
        self.core = self.n % 2
        self.y = self.n // 2
        other_w = self.w + 1 - 2 * self.x
        other_n = self.n + 2 - 4 * self.y
        self.first = self.mix((other_w, self.n), (self.w, other_n))
        self.second = self.mix((self.w, other_n), (other_w, self.n))
        self.twin = (self.w, self.n + 1 - 2 * self.core)
        self.along_x = (other_w, self.n)
        self.along_y = (self.w, other_n)

    def mix(self, zero, one):
        return tuple((1 - self.core) * a + self.core * b for a, b in zip(zero, one))

    def line(self, z):
        return (2 * z + self.x, self.n)

    def partners(self):
        found = [self.twin, self.first, self.second]
        for step in range(1, self.levels):
            found.append(self.line((self.z + step) % self.levels))
        return found

    def rows(self, w, n):
        return pl.ds(pl.multiple_of((w * self.narrow + n) * self.share, 16), self.share)

    def shards(self, z):
        out = []
        for n, n_first, n_second, w_first, w_second in (
            (self.n, self.first[1], self.second[1], self.first[0], self.second[0]),
            (
                self.twin[1],
                self.twin[1] + (1 - self.core) * (2 - 4 * self.y),
                self.twin[1] + self.core * (2 - 4 * self.y),
                self.w + self.core * (1 - 2 * self.x),
                self.w + (1 - self.core) * (1 - 2 * self.x),
            ),
        ):
            cross = n + 2 - 4 * self.y
            out.append(self.rows(2 * z + self.x, n))
            out.append(self.rows(2 * z + w_first % 2, n_first))
            out.append(self.rows(2 * z + w_second % 2, n_second))
            out.append(self.rows(2 * z + 1 - self.x, cross))
        return out


def send(source, target, send_sem, recv_sem, device):
    return pltpu.make_async_remote_copy(
        src_ref=source,
        dst_ref=target,
        send_sem=send_sem,
        recv_sem=recv_sem,
        device_id=device,
        device_id_type=MESH,
    )


def kernel(wide, narrow, linked, tok, seg, mats, vec, cot, *refs):
    out, grad_in, mat_out, vec_out, park_u, park_s, park_n, park_g = refs[:8]
    (
        weights,
        grads,
        landing,
        u,
        gp,
        s,
        n,
        tmp,
        a,
        xf,
        xb,
        masked,
        masked_t,
        rstd_in,
        rstd_mid,
        acc1,
        acc2,
        seg_t,
        bias_t,
        bias_sum,
        gains,
        inv_gains,
        vec_sum,
        vec_in,
        local_sem,
        credit,
        g_send,
        g_recv,
        r_send,
        r_recv,
        v_send,
        v_recv,
    ) = refs[8:]
    tokens = xf.shape[0]
    rows_here = tokens // S
    share = mats.shape[1]
    links = Links(wide, narrow, share) if linked else None
    levels = wide // 2
    passed_on, started = ([], []), []

    load_tok = pltpu.make_async_copy(tok, xb, local_sem.at[0])
    load_tok.start()
    load_mats = []
    for layer in range(LAYERS):
        place = links.rows(links.w, links.n) if linked else pl.ds(0, ALL_ROWS)
        copy = pltpu.make_async_copy(
            mats.at[layer], weights.at[layer, place], local_sem.at[1 + layer]
        )
        copy.start()
        load_mats.append(copy)

    if linked:
        barrier = pltpu.get_barrier_semaphore()
        for device in links.partners():
            pl.semaphore_signal(barrier, inc=1, device_id=device, device_id_type=MESH)
        pl.semaphore_wait(barrier, len(links.partners()))

    def pass_on(layer, z, slot, rows, target_slot, send_slot, device):
        copy = send(
            weights.at[layer, rows],
            weights.at[layer, rows],
            g_send.at[layer, z, send_slot],
            g_recv.at[layer, z, target_slot],
            device,
        )
        copy.start()
        passed_on[layer].append(copy)

    def arrived(layer, z, slot, rows):
        send(
            weights.at[layer, rows],
            weights.at[layer, rows],
            g_send.at[layer, z, 0],
            g_recv.at[layer, z, slot],
            links.twin,
        ).wait_recv()

    def gather_own(layer):
        load_mats[layer].wait()
        shards = links.shards(links.z)
        for step in range(1, levels):
            copy = send(
                weights.at[layer, shards[0]],
                weights.at[layer, shards[0]],
                g_send.at[layer, step, 7],
                g_recv.at[layer, links.z, 0],
                links.line((links.z + step) % levels),
            )
            copy.start()
            passed_on[layer].append(copy)
        gather_from_line(layer, 0)

    def gather_from_line(layer, step):
        z = (links.z + step) % levels
        shards = links.shards(z)
        if step:
            arrived(layer, z, 0, shards[0])
        pass_on(layer, z, 0, shards[0], 1, 0, links.first)
        pass_on(layer, z, 0, shards[0], 2, 1, links.second)
        pass_on(layer, z, 0, shards[0], 4, 3, links.twin)

    def gather_from_first(layer, step):
        z = (links.z + step) % levels
        shards = links.shards(z)
        arrived(layer, z, 1, shards[1])
        pass_on(layer, z, 1, shards[1], 3, 2, links.second)
        pass_on(layer, z, 1, shards[1], 5, 4, links.twin)

    def gather_from_second(layer, step):
        z = (links.z + step) % levels
        shards = links.shards(z)
        for slot in (2, 3):
            arrived(layer, z, slot, shards[slot])
            pass_on(layer, z, slot, shards[slot], 4 + slot, 3 + slot, links.twin)

    def gather_from_twin(layer, step):
        z = (links.z + step) % levels
        shards = links.shards(z)
        for slot in range(4, 8):
            arrived(layer, z, slot, shards[slot])

    def gather_all(layer, parts):
        for part in parts:
            for step in range(levels):
                if part is not gather_from_line or step:
                    part(layer, step)

    def land(layer, index):
        rows = pl.ds(pl.multiple_of(index * share, 16), share)
        return weights.at[1, rows] if layer == 0 else landing.at[rows]

    def add_in(layer, rows, index):
        grads[layer, rows, :] = (
            grads[layer, rows, :].astype(F32) + land(layer, index)[...].astype(F32)
        ).astype(BF16)

    def reduce_copy(layer, z, rows, target, slot, device, recv_z=None):
        return send(
            grads.at[layer, rows],
            land(layer, target),
            r_send.at[layer, z, slot],
            r_recv.at[layer, z if recv_z is None else recv_z, slot],
            device,
        )

    def reduce_begin(layer, z):
        shards = links.shards(z)
        for slot in range(4):
            copy = reduce_copy(layer, z, shards[4 + slot], 4 * z + slot, slot, links.twin)
            copy.start()
            started.append(copy)

    def reduce_second(layer, z):
        shards = links.shards(z)
        for slot in (2, 3, 0, 1):
            reduce_copy(layer, z, shards[slot], 4 * z + slot, slot, links.twin).wait_recv()
            add_in(layer, shards[slot], 4 * z + slot)
            if slot >= 2:
                copy = reduce_copy(
                    layer, z, shards[slot], 4 * levels + 2 * z + slot - 2, 2 + slot, links.second
                )
                copy.start()
                started.append(copy)

    def reduce_first(layer, z):
        shards = links.shards(z)
        for slot in (1, 0):
            index = 4 * levels + 2 * z + slot
            reduce_copy(layer, z, shards[slot], index, 4 + slot, links.second).wait_recv()
            add_in(layer, shards[slot], index)
            if slot == 1:
                copy = reduce_copy(layer, z, shards[1], 6 * levels + z, 6, links.first)
                copy.start()
                started.append(copy)

    def line_copy(layer, z):
        return reduce_copy(
            layer, z, links.shards(z)[0], 7 * levels + links.z, 7, links.line(z), links.z
        )

    def reduce_line(layer, z):
        shards = links.shards(z)
        index = 6 * levels + z
        reduce_copy(layer, z, shards[0], index, 6, links.first).wait_recv()
        add_in(layer, shards[0], index)

        @pl.when(links.z != z)
        def _():
            line_copy(layer, z).start()

    def reduce_end(layer):
        shards = links.shards(links.z)
        total = grads[layer, shards[0], :].astype(F32)
        for step in range(1, levels):
            z = (links.z + step) % levels
            reduce_copy(layer, z, shards[0], 7 * levels + z, 7, links.line(z)).wait_recv()
            total = total + land(layer, 7 * levels + z)[...].astype(F32)
        mat_out[layer] = total
        for z in range(levels):

            @pl.when(links.z != z)
            def _():
                line_copy(layer, z).wait_send()

    gains[...] = vec[...].astype(F32)
    inv_gains[...] = 1.0 / gains[...]
    for r in range(rows_here):
        line = jnp.broadcast_to(seg[r : r + 1, :].astype(F32), (128, S))
        seg_t[r] = line.T

    def same(r):
        return lanes(seg_t[r], S) == seg[r : r + 1, :].astype(F32)

    def row_chunk(i, size):
        return pl.ds(pl.multiple_of(i * size, size), size)

    def norm_in(layer):
        gain = gains[layer : layer + 1, :D]

        @pl.loop(0, tokens // 128)
        def _(i):
            rows = row_chunk(i, 128)
            values = xb[rows, :].astype(F32) if layer == 0 else xf[rows, :]
            center = values - jnp.mean(values, axis=1, keepdims=True)
            scale = lax.rsqrt(jnp.mean(center * center, axis=1, keepdims=True) + EPSILON)
            a[layer, rows, :] = (center * scale * gain).astype(BF16)
            rstd_in[layer, rows, :] = jnp.broadcast_to(scale, (128, 128))

    def hidden_gate(layer):
        @pl.loop(0, HALF // BLOCK)
        def _(i):
            cols = row_chunk(i, BLOCK)
            for r in range(rows_here):
                rows = pl.ds(r * S, S)
                z = dot(a[layer, rows, :], weights[layer, cols, :], 1, 1)
                value, slope = gelu_and_slope(z)
                u[rows, cols] = value.astype(BF16)
                gp[rows, cols] = slope.astype(BF16)

    def hidden_value(layer):
        acc1[...] = jnp.zeros_like(acc1)

        @pl.loop(0, HALF // BLOCK)
        def _(i):
            cols = row_chunk(i, BLOCK)
            cols_all = pl.ds(pl.multiple_of(HALF + i * BLOCK, BLOCK), BLOCK)
            for r in range(rows_here):
                rows = pl.ds(r * S, S)
                z = dot(a[layer, rows, :], weights[layer, cols_all, :], 1, 1)
                value, slope = gelu_and_slope(z)
                n[rows, cols] = value.astype(BF16)
                gp[rows, cols_all] = slope.astype(BF16)
                acc1[rows, :] += lane_groups(value)

    def norm_mid(layer):
        gain = gains[layer : layer + 1, D : D + HALF]

        @pl.loop(0, tokens // 64)
        def _(i):
            rows = row_chunk(i, 64)
            mean = jnp.sum(acc1[rows, :], axis=1, keepdims=True) * (1.0 / HALF)
            center = n[rows, :].astype(F32) - mean
            scale = lax.rsqrt(jnp.mean(center * center, axis=1, keepdims=True) + EPSILON)
            n[rows, :] = (center * scale * gain).astype(BF16)
            rstd_mid[layer, rows, :] = jnp.broadcast_to(scale, (64, 128))

    def mask_weights(layer):
        spatial = weights[layer, FF + HALF :, :].astype(F32)
        spatial_t = spatial.T
        for r in range(rows_here):
            keep = same(r)
            masked[r] = jnp.where(keep, spatial, 0.0).astype(BF16)
            masked_t[r] = jnp.where(keep, spatial_t, 0.0).astype(BF16)
        line = jnp.broadcast_to(gains[layer : layer + 1, D + HALF :], (128, S))
        bias_t[...] = line.T

    def mix(layer):
        @pl.loop(0, HALF // BLOCK)
        def _(i):
            cols = row_chunk(i, BLOCK)
            for r in range(rows_here):
                rows = pl.ds(r * S, S)
                mixed = dot(masked[r], n[rows, cols], 1, 0) + lanes(bias_t[...], BLOCK)
                s[rows, cols] = mixed.astype(BF16)
                tmp[rows, cols] = (u[rows, cols].astype(F32) * mixed).astype(BF16)

    def project(layer):
        @pl.loop(0, tokens // S)
        def _(i):
            rows = row_chunk(i, S)
            values = xb[rows, :].astype(F32) if layer == 0 else xf[rows, :]
            xf[rows, :] = values + dot(tmp[rows, :], weights[layer, FF : FF + HALF, :], 1, 0)

    def back_project(layer):
        bias_sum[...] = jnp.zeros_like(bias_sum)

        @pl.loop(0, HALF // BLOCK)
        def _(i):
            cols = row_chunk(i, BLOCK)
            w_rows = pl.ds(pl.multiple_of(FF + i * BLOCK, BLOCK), BLOCK)
            for r in range(rows_here):
                rows = pl.ds(r * S, S)
                dy = dot(xb[rows, :], weights[layer, w_rows, :], 1, 1)
                gate = u[rows, cols].astype(F32)
                mixed = s[rows, cols].astype(F32)
                ds = (dy * gate).astype(BF16)
                u[rows, cols] = (gate * mixed).astype(BF16)
                s[rows, cols] = ds
                gp[rows, cols] = (dy * mixed * gp[rows, cols].astype(F32)).astype(BF16)
                bias_sum[...] += lane_groups(ds.astype(F32))
            grads[layer, w_rows, :] = dot(u[:, cols], xb[...], 0, 0).astype(BF16)

    def back_input_weights(layer, low, high):
        @pl.loop(low, high)
        def _(i):
            cols = row_chunk(i, BLOCK)
            grads[layer, cols, :] = dot(gp[:, cols], a[layer], 0, 0).astype(BF16)

    def back_spatial(layer):
        total = None
        for r in range(rows_here):
            rows = pl.ds(r * S, S)
            outer = jnp.where(same(r), dot(s[rows, :], n[rows, :], 1, 1), 0.0)
            total = outer if total is None else total + outer
        grads[layer, FF + HALF :, :] = total.astype(BF16)
        at = layer * VEC + D + HALF
        vec_sum[:, at : at + S] = jnp.sum(bias_sum[...].T, axis=0, keepdims=True)

    def back_mix(layer):
        acc1[...] = jnp.zeros_like(acc1)
        acc2[...] = jnp.zeros_like(acc2)

        @pl.loop(0, HALF // BLOCK)
        def _(i):
            cols = row_chunk(i, BLOCK)
            at = pl.ds(pl.multiple_of(D + i * BLOCK, BLOCK), BLOCK)
            to = pl.ds(pl.multiple_of(layer * VEC + D + i * BLOCK, BLOCK), BLOCK)
            column = jnp.zeros((1, BLOCK), F32)
            for r in range(rows_here):
                rows = pl.ds(r * S, S)
                dn = dot(masked_t[r], s[rows, cols], 1, 0)
                e = dn * gains[layer : layer + 1, at]
                dn_n = dn * n[rows, cols].astype(F32)
                tmp[rows, cols] = e.astype(BF16)
                acc1[rows, :] += lane_groups(e)
                acc2[rows, :] += lane_groups(dn_n)
                column = column + jnp.sum(dn_n, axis=0, keepdims=True)
            vec_sum[:, to] = column * inv_gains[layer : layer + 1, at]

    def back_norm_mid(layer):
        inverse = inv_gains[layer : layer + 1, D : D + HALF]

        @pl.loop(0, tokens // 64)
        def _(i):
            rows = row_chunk(i, 64)
            mean_e = jnp.sum(acc1[rows, :], axis=1, keepdims=True) * (1.0 / HALF)
            mean_ew = jnp.sum(acc2[rows, :], axis=1, keepdims=True) * (1.0 / HALF)
            w = n[rows, :].astype(F32) * inverse
            dv = tmp[rows, :].astype(F32) - mean_e - w * mean_ew
            dv = dv * lanes(rstd_mid[layer, rows, :], HALF)
            gp[rows, HALF:] = (dv * gp[rows, HALF:].astype(F32)).astype(BF16)

    def back_input(layer):
        gain = gains[layer : layer + 1, :D]
        inverse = inv_gains[layer : layer + 1, :D]
        at = layer * VEC
        vec_sum[:, at : at + D] = jnp.zeros((1, D), F32)

        @pl.loop(0, tokens // S)
        def _(i):
            rows = row_chunk(i, S)
            da = dot(gp[rows, :], weights[layer, :FF, :], 1, 0)
            normed = a[layer, rows, :].astype(F32)
            product = da * normed
            e = da * gain
            mean_e = jnp.mean(e, axis=1, keepdims=True)
            mean_ew = jnp.mean(product, axis=1, keepdims=True)
            dx = (e - mean_e - normed * inverse * mean_ew) * lanes(rstd_in[layer, rows, :], D)
            upper = xb[rows, :].astype(F32) if layer == LAYERS - 1 else xf[rows, :]
            total = upper + dx
            xf[rows, :] = total
            if layer:
                xb[rows, :] = total.astype(BF16)
            vec_sum[:, at : at + D] += jnp.sum(product, axis=0, keepdims=True) * inverse

    parts = (gather_from_line, gather_from_first, gather_from_second, gather_from_twin)
    if linked:
        gather_own(0)
    load_tok.wait()
    norm_in(0)
    if linked:
        gather_all(0, parts[:1])
        gather_own(1)
        gather_all(0, parts[1:])
    else:
        load_mats[0].wait()
    hidden_gate(0)
    keep_u = pltpu.make_async_copy(u, park_u, local_sem.at[3])
    keep_u.start()
    if linked:
        gather_all(1, parts[:1])
    hidden_value(0)
    keep_g = pltpu.make_async_copy(gp, park_g, local_sem.at[4])
    keep_g.start()
    if linked:
        gather_all(1, parts[1:2])
    mask_weights(0)
    norm_mid(0)
    keep_n = pltpu.make_async_copy(n, park_n, local_sem.at[5])
    keep_n.start()
    mix(0)
    keep_s = pltpu.make_async_copy(s, park_s, local_sem.at[6])
    keep_s.start()
    if linked:
        gather_all(1, parts[2:3])
    project(0)
    load_cot = pltpu.make_async_copy(cot, xb, local_sem.at[0])
    load_cot.start()
    norm_in(1)
    if linked:
        gather_all(1, parts[3:])
    else:
        load_mats[1].wait()
    keep_u.wait()
    keep_g.wait()
    hidden_gate(1)
    keep_n.wait()
    hidden_value(1)
    mask_weights(1)
    norm_mid(1)
    keep_s.wait()
    mix(1)
    project(1)
    write_out = pltpu.make_async_copy(xf, out, local_sem.at[1])
    write_out.start()
    load_cot.wait()

    back_project(1)
    back_input_weights(1, 0, HALF // BLOCK)
    load_u = pltpu.make_async_copy(park_u, u, local_sem.at[3])
    load_u.start()
    if linked:
        reduce_begin(1, 0)
    back_spatial(1)
    if linked:
        reduce_begin(1, levels - 1)
        reduce_second(1, 0)
    back_mix(1)
    load_s = pltpu.make_async_copy(park_s, s, local_sem.at[6])
    load_s.start()
    if linked:
        reduce_second(1, levels - 1)
    back_norm_mid(1)
    load_n = pltpu.make_async_copy(park_n, n, local_sem.at[5])
    load_n.start()
    if linked:
        reduce_first(1, 0)
    back_input_weights(1, HALF // BLOCK, FF // BLOCK)
    if linked:
        for z in range(levels - 2, 0, -1):
            reduce_begin(1, z)
        reduce_first(1, levels - 1)
        reduce_line(1, 0)
    write_out.wait()
    back_input(1)
    load_g = pltpu.make_async_copy(park_g, gp, local_sem.at[4])
    load_g.start()
    if linked:
        for copy in passed_on[1]:
            copy.wait_send()
        for device in links.partners():
            pl.semaphore_signal(credit, inc=1, device_id=device, device_id_type=MESH)
        reduce_line(1, levels - 1)
        for z in range(levels - 2, 0, -1):
            reduce_second(1, z)

    mask_weights(0)
    load_u.wait()
    load_s.wait()
    load_g.wait()
    back_project(0)
    if linked:
        for z in range(levels - 2, 0, -1):
            reduce_first(1, z)
    back_input_weights(0, 0, HALF // BLOCK)
    if linked:
        pl.semaphore_wait(credit, len(links.partners()))
        reduce_begin(0, 0)
        for z in range(levels - 2, 0, -1):
            reduce_line(1, z)
    load_n.wait()
    back_spatial(0)
    if linked:
        reduce_begin(0, levels - 1)
        reduce_second(0, 0)
        reduce_end(1)
    back_mix(0)
    if linked:
        reduce_second(0, levels - 1)
        reduce_first(0, 0)
    back_norm_mid(0)
    back_input_weights(0, HALF // BLOCK, FF // BLOCK)
    if linked:
        for z in range(levels - 2, 0, -1):
            reduce_begin(0, z)
        reduce_first(0, levels - 1)
        reduce_line(0, 0)
        for z in range(levels - 2, 0, -1):
            reduce_second(0, z)
        reduce_line(0, levels - 1)
    back_input(0)
    write_in = pltpu.make_async_copy(xf, grad_in, local_sem.at[0])
    write_in.start()
    if linked:
        for z in range(levels - 2, 0, -1):
            reduce_first(0, z)
        for index, device in ((0, links.twin), (1, links.along_y), (2, links.along_x)):
            copy = send(
                vec_sum, vec_in.at[levels + index], v_send.at[index], v_recv.at[index], device
            )
            copy.start()
            copy.wait()
            vec_sum[...] = vec_sum[...] + vec_in[levels + index]
        copies = []
        for step in range(1, levels):
            z = (links.z + step) % levels
            copy = send(
                vec_sum, vec_in.at[links.z], v_send.at[2 + step], v_recv.at[3 + links.z], links.line(z)
            )
            copy.start()
            copies.append(copy)
        for z in range(levels - 2, 0, -1):
            reduce_line(0, z)
        for step in range(1, levels):
            z = (links.z + step) % levels
            send(
                vec_sum, vec_in.at[z], v_send.at[2 + step], v_recv.at[3 + z], links.line(z)
            ).wait_recv()
        for copy in copies:
            copy.wait_send()
        vec_in[pl.ds(links.z, 1)] = vec_sum[...][None]
        total = vec_in[0]
        for z in range(1, levels):
            total = total + vec_in[z]
        reduce_end(0)
        for copy in passed_on[0] + started:
            copy.wait_send()
    else:
        total = vec_sum[...]
        for layer in range(LAYERS):
            copy = pltpu.make_async_copy(grads.at[layer], mat_out.at[layer], local_sem.at[1])
            copy.start()
            copy.wait()
    for layer in range(LAYERS):
        vec_out[layer : layer + 1, :] = total[:, layer * VEC : (layer + 1) * VEC]
    write_in.wait()


def per_device(wide, narrow, tokens, segment_ids, matrices, vectors, cotangent):
    axes = ("wide", "narrow")
    count, share = tokens.shape[0], matrices.shape[1]
    total = count * S
    linked = narrow == 4 and wide % 2 == 0 and wide >= 8 and share % 16 == 0
    if not linked:
        matrices = lax.all_gather(matrices, axes, axis=1, tiled=True)
    levels = wide // 2
    anywhere = pl.BlockSpec(memory_space=pl.ANY)
    vmem = pl.BlockSpec(memory_space=pltpu.VMEM)
    mat_shape = (LAYERS, share, D) if linked else (LAYERS, ALL_ROWS, D)
    half, full = (total, HALF), (total, FF)
    dma = pltpu.SemaphoreType.DMA
    flags = dict(collective_id=0) if linked else {}
    results = pl.pallas_call(
        functools.partial(kernel, wide, narrow, linked),
        out_shape=(
            jax.ShapeDtypeStruct((total, D), F32),
            jax.ShapeDtypeStruct((total, D), F32),
            jax.ShapeDtypeStruct(mat_shape, F32 if linked else BF16),
            jax.ShapeDtypeStruct((LAYERS, VEC), F32),
            jax.ShapeDtypeStruct(half, BF16),
            jax.ShapeDtypeStruct(half, BF16),
            jax.ShapeDtypeStruct(half, BF16),
            jax.ShapeDtypeStruct(full, BF16),
        ),
        in_specs=[anywhere, vmem, anywhere, vmem, anywhere],
        out_specs=(anywhere, anywhere, vmem if linked else anywhere, vmem) + (anywhere,) * 4,
        scratch_shapes=[
            pltpu.VMEM((LAYERS, ALL_ROWS, D), BF16),
            pltpu.VMEM((LAYERS, ALL_ROWS, D), BF16),
            pltpu.VMEM((ALL_ROWS if linked else 16, D), BF16),
            pltpu.VMEM(half, BF16),
            pltpu.VMEM(full, BF16),
            pltpu.VMEM(half, BF16),
            pltpu.VMEM(half, BF16),
            pltpu.VMEM(half, BF16),
            pltpu.VMEM((LAYERS, total, D), BF16),
            pltpu.VMEM((total, D), F32),
            pltpu.VMEM((total, D), BF16),
            pltpu.VMEM((count, S, S), BF16),
            pltpu.VMEM((count, S, S), BF16),
            pltpu.VMEM((LAYERS, total, 128), F32),
            pltpu.VMEM((LAYERS, total, 128), F32),
            pltpu.VMEM((total, 128), F32),
            pltpu.VMEM((total, 128), F32),
            pltpu.VMEM((count, S, 128), F32),
            pltpu.VMEM((S, 128), F32),
            pltpu.VMEM((S, 128), F32),
            pltpu.VMEM((LAYERS, VEC), F32),
            pltpu.VMEM((LAYERS, VEC), F32),
            pltpu.VMEM((1, LAYERS * VEC), F32),
            pltpu.VMEM((levels + 3, 1, LAYERS * VEC), F32),
            dma((7,)),
            pltpu.SemaphoreType.REGULAR,
            dma((LAYERS, levels, 8)),
            dma((LAYERS, levels, 8)),
            dma((LAYERS, levels, 8)),
            dma((LAYERS, levels, 8)),
            dma((levels + 3,)),
            dma((levels + 3,)),
        ],
        compiler_params=pltpu.CompilerParams(
            has_side_effects=True, vmem_limit_bytes=63 << 20, **flags
        ),
    )(
        tokens.reshape(total, D),
        segment_ids,
        matrices,
        vectors,
        cotangent.reshape(total, D),
    )
    out, grad_in, mat_grads, vec_grads = results[:4]
    if not linked:
        mat_grads = lax.psum_scatter(
            mat_grads.astype(F32), axes, scatter_dimension=1, tiled=True
        )
        vec_grads = lax.psum(vec_grads, axes)
    return (out.reshape(tokens.shape), grad_in.reshape(tokens.shape), mat_grads, vec_grads)


def solution(mesh):
    rows = P(("wide", "narrow"), None, None)
    spread = P(None, ("wide", "narrow"), None)
    return jax.shard_map(
        functools.partial(per_device, mesh.shape["wide"], mesh.shape["narrow"]),
        mesh=mesh,
        in_specs=(rows, P(("wide", "narrow"), None), spread, P(), rows),
        out_specs=(rows, rows, spread, P()),
        check_vma=False,
    )
```

```python
import functools

import jax
import jax.numpy as jnp
from jax import lax
from jax.experimental import pallas as pl
from jax.experimental.pallas import tpu as pltpu
from jax.sharding import PartitionSpec as P

D = 512
FF = 3072
HALF = FF // 2
S = 512
LAYERS = 2
VEC = D + HALF + S
ALL_ROWS = FF + HALF + S
EPSILON = 1e-05
BLOCK = 512
PART = 256
WIDTH = 256
MESH = pl.DeviceIdType.MESH
BF16 = jnp.bfloat16
F32 = jnp.float32
GELU_A = 0.7978845608028654
GELU_B = 0.044715


def dot(left, right, left_dim, right_dim):
    dims = (((left_dim,), (right_dim,)), ((), ()))
    return lax.dot_general(left, right, dims, preferred_element_type=F32)


def gelu_and_slope(z):
    squared = z * z
    share = 0.5 + 0.5 * jnp.tanh(z * (GELU_A + (GELU_A * GELU_B) * squared))
    value = z * share
    near, gate = value.astype(BF16), share.astype(BF16)
    rise = BF16(2.0 * GELU_A) + BF16(6.0 * GELU_A * GELU_B) * squared.astype(BF16)
    return value, gate + (near - near * gate) * rise


def lane_groups(values):
    total = values[:, :128]
    for at in range(128, values.shape[1], 128):
        total = total + values[:, at : at + 128]
    return total


def lanes(column, width):
    return jnp.concatenate([column] * (width // 128), axis=1)


class Links:
    def __init__(self, wide, narrow, share):
        self.share = share
        self.levels = wide // 2
        self.narrow = narrow
        self.w = lax.axis_index("wide")
        self.n = lax.axis_index("narrow")
        self.x = self.w % 2
        self.z = self.w // 2
        self.core = self.n % 2
        self.y = self.n // 2
        other_w = self.w + 1 - 2 * self.x
        other_n = self.n + 2 - 4 * self.y
        self.first = self.mix((other_w, self.n), (self.w, other_n))
        self.second = self.mix((self.w, other_n), (other_w, self.n))
        self.twin = (self.w, self.n + 1 - 2 * self.core)
        self.along_x = (other_w, self.n)
        self.along_y = (self.w, other_n)

    def mix(self, zero, one):
        return tuple((1 - self.core) * a + self.core * b for a, b in zip(zero, one))

    def line(self, z):
        return (2 * z + self.x, self.n)

    def partners(self):
        found = [self.twin, self.first, self.second]
        for step in range(1, self.levels):
            found.append(self.line((self.z + step) % self.levels))
        return found

    def rows(self, w, n):
        return pl.ds(pl.multiple_of((w * self.narrow + n) * self.share, 16), self.share)

    def shards(self, z):
        out = []
        for n, n_first, n_second, w_first, w_second in (
            (self.n, self.first[1], self.second[1], self.first[0], self.second[0]),
            (
                self.twin[1],
                self.twin[1] + (1 - self.core) * (2 - 4 * self.y),
                self.twin[1] + self.core * (2 - 4 * self.y),
                self.w + self.core * (1 - 2 * self.x),
                self.w + (1 - self.core) * (1 - 2 * self.x),
            ),
        ):
            cross = n + 2 - 4 * self.y
            out.append(self.rows(2 * z + self.x, n))
            out.append(self.rows(2 * z + w_first % 2, n_first))
            out.append(self.rows(2 * z + w_second % 2, n_second))
            out.append(self.rows(2 * z + 1 - self.x, cross))
        return out


def send(source, target, send_sem, recv_sem, device):
    return pltpu.make_async_remote_copy(
        src_ref=source,
        dst_ref=target,
        send_sem=send_sem,
        recv_sem=recv_sem,
        device_id=device,
        device_id_type=MESH,
    )


def kernel(wide, narrow, linked, tok, seg, mats, vec, cot, *refs):
    out, grad_in, mat_out, vec_out, park_u, park_s, park_n, park_g = refs[:8]
    (
        weights,
        grads,
        landing,
        u,
        gp,
        s,
        n,
        a,
        xf,
        xb,
        masked,
        masked_t,
        rstd_in,
        rstd_mid,
        acc1,
        acc2,
        vf,
        mat_stage,
        seg_t,
        bias_t,
        bias_sum,
        gains,
        inv_gains,
        vec_sum,
        vec_in,
        local_sem,
        credit,
        g_send,
        g_recv,
        r_send,
        r_recv,
        v_send,
        v_recv,
    ) = refs[8:]
    tokens = xf.shape[0]
    rows_here = tokens // S
    share = mats.shape[1]
    links = Links(wide, narrow, share) if linked else None
    levels = wide // 2 if linked else 4
    passed_on, started = ([], []), []

    load_tok = pltpu.make_async_copy(tok, xb, local_sem.at[0])
    load_tok.start()
    load_mats = []
    for layer in range(LAYERS):
        place = links.rows(links.w, links.n) if linked else pl.ds(0, ALL_ROWS)
        copy = pltpu.make_async_copy(
            mats.at[layer], weights.at[layer, place], local_sem.at[1 + layer]
        )
        copy.start()
        load_mats.append(copy)

    if linked:
        barrier = pltpu.get_barrier_semaphore()
        for device in links.partners():
            pl.semaphore_signal(barrier, inc=1, device_id=device, device_id_type=MESH)
        pl.semaphore_wait(barrier, len(links.partners()))

    if linked:
        sources, targets = [], []
        for step in range(levels):
            below = (links.z - step + 2 * levels) // (2 * levels)
            sources.append(below * (links.z - step) + (1 - below) * step)
        for step in range(1, levels):
            above = (levels - 1 - links.z - step + 2 * levels) // (2 * levels)
            upward = links.z + step
            downward = levels - 1 - step
            targets.append(links.line(above * upward + (1 - above) * downward))
        not_top = links.z < levels - 1
        shards_of = [links.shards(z) for z in sources]

    def gather_copy(layer, step, slot, send_slot, target_slot, device):
        rows = shards_of[step][slot]
        return send(
            weights.at[layer, rows],
            weights.at[layer, rows],
            g_send.at[layer, sources[step], send_slot],
            g_recv.at[layer, sources[step], target_slot],
            device,
        )

    def pass_on(layer, step, slot, send_slot, target_slot, device):
        again = functools.partial(gather_copy, layer, step, slot, send_slot, target_slot, device)
        again().start()
        passed_on[layer].append(again)

    def arrived(layer, step, slot):
        gather_copy(layer, step, slot, 0, slot, links.twin).wait_recv()

    def gather_depart(layer):
        load_mats[layer].wait()
        for at, device in enumerate(targets):
            pass_on(layer, 0, 0, 7 + at, 0, device)

    def gather_line(layer, step):
        if step:
            arrived(layer, step, 0)
        pass_on(layer, step, 0, 0, 1, links.first)
        pass_on(layer, step, 0, 1, 2, links.second)
        pass_on(layer, step, 0, 3, 4, links.twin)

    def gather_first(layer, step):
        arrived(layer, step, 1)
        pass_on(layer, step, 1, 2, 3, links.second)
        pass_on(layer, step, 1, 4, 5, links.twin)

    def gather_second(layer, step):
        for slot in (2, 3):
            arrived(layer, step, slot)
            pass_on(layer, step, slot, 3 + slot, 4 + slot, links.twin)

    def gather_twin(layer, step):
        for slot in range(4, 8):
            arrived(layer, step, slot)

    def gather_sent(layer):
        for again in passed_on[layer]:
            again().wait_send()

    if linked:
        shards_at = [links.shards(z) for z in range(levels)]
        own_shards = links.shards(links.z)

    def land(layer, index):
        rows = pl.ds(pl.multiple_of(index * share, 16), share)
        return weights.at[1, rows] if layer == 0 else landing.at[rows]

    def add_in(layer, rows, index):
        grads[layer, rows, :] = (
            grads[layer, rows, :].astype(F32) + land(layer, index)[...].astype(F32)
        ).astype(BF16)

    def reduce_copy(layer, z, rows, target, slot, device, recv_z=None):
        return send(
            grads.at[layer, rows],
            land(layer, target),
            r_send.at[layer, z, slot],
            r_recv.at[layer, z if recv_z is None else recv_z, slot],
            device,
        )

    def reduce_start(*where):
        reduce_copy(*where).start()
        started.append(where)

    def reduce_begin(layer, z):
        shards = shards_at[z]
        for slot in range(4):
            reduce_start(layer, z, shards[4 + slot], 4 * z + slot, slot, links.twin)

    def reduce_second(layer, z):
        shards = shards_at[z]
        for slot in (2, 3, 0, 1):
            reduce_copy(layer, z, shards[slot], 4 * z + slot, slot, links.twin).wait_recv()
            add_in(layer, shards[slot], 4 * z + slot)
            if slot >= 2:
                index = 4 * levels + 2 * z + slot - 2
                reduce_start(layer, z, shards[slot], index, 2 + slot, links.second)

    def reduce_first(layer, z):
        shards = shards_at[z]
        for slot in (1, 0):
            index = 4 * levels + 2 * z + slot
            reduce_copy(layer, z, shards[slot], index, 4 + slot, links.second).wait_recv()
            add_in(layer, shards[slot], index)
            if slot == 1:
                reduce_start(layer, z, shards[1], 6 * levels + z, 6, links.first)

    def line_copy(layer, z):
        return reduce_copy(
            layer, z, shards_at[z][0], 7 * levels + links.z, 7, links.line(z), links.z
        )

    def reduce_line(layer, z):
        shards = shards_at[z]
        index = 6 * levels + z
        reduce_copy(layer, z, shards[0], index, 6, links.first).wait_recv()
        add_in(layer, shards[0], index)

        @pl.when(links.z != z)
        def _():
            line_copy(layer, z).start()

    def mat_copy(layer):
        return pltpu.make_async_copy(mat_stage.at[layer], mat_out.at[layer], local_sem.at[1 + layer])

    def reduce_end(layer):
        shards = own_shards
        total = grads[layer, shards[0], :].astype(F32)
        for step in range(1, levels):
            z = (links.z + step) % levels
            reduce_copy(layer, z, shards[0], 7 * levels + z, 7, links.line(z)).wait_recv()
            total = total + land(layer, 7 * levels + z)[...].astype(F32)
        mat_stage[layer] = total
        mat_copy(layer).start()
        for z in range(levels):

            @pl.when(links.z != z)
            def _():
                line_copy(layer, z).wait_send()

    def vec_pair(index, device):
        return send(vec_sum, vec_in.at[levels + index], v_send.at[index], v_recv.at[index], device)

    def vec_add(index, device):
        vec_pair(index, device).wait()
        vec_sum[...] = vec_sum[...] + vec_in[levels + index]

    def vec_copy(step, z):
        return send(
            vec_sum,
            vec_in.at[z],
            v_send.at[2 + step],
            v_recv.at[3 + z],
            links.line((links.z + step) % levels),
        )

    def vec_line_begin():
        for step in range(1, levels):
            vec_copy(step, links.z).start()

    def vec_line_end():
        for step in range(1, levels):
            vec_copy(step, (links.z + step) % levels).wait_recv()
        for step in range(1, levels):
            vec_copy(step, links.z).wait_send()
        vec_in[pl.ds(links.z, 1)] = vec_sum[...][None]
        total = vec_in[0]
        for z in range(1, levels):
            total = total + vec_in[z]
        return total

    def prepare():
        gains[...] = vec[...].astype(F32)
        inv_gains[...] = 1.0 / gains[...]
        for r in range(rows_here):
            line = jnp.broadcast_to(seg[r : r + 1, :].astype(F32), (128, S))
            seg_t[r] = line.T
        acc1[...] = jnp.zeros_like(acc1)

    def same(r):
        return lanes(seg_t[r], S) == seg[r : r + 1, :].astype(F32)

    def row_chunk(i, size):
        return pl.ds(pl.multiple_of(i * size, size), size)

    def between(i, hooks):
        for at, hook in enumerate(hooks):
            if hook is not None:
                pl.when(i == at)(hook)

    def norm_in(layer):
        gain = gains[layer : layer + 1, :D]

        @pl.loop(0, tokens // 256)
        def _(i):
            found = []
            for part in range(2):
                rows = row_chunk(2 * i + part, 128)
                values = xb[rows, :].astype(F32) if layer == 0 else xf[rows, :]
                mean = jnp.sum(lane_groups(values), axis=1, keepdims=True) * (1.0 / D)
                found.append((rows, values - mean))
            for at, (rows, center) in enumerate(found):
                spread = jnp.sum(lane_groups(center * center), axis=1, keepdims=True) * (1.0 / D)
                found[at] = (rows, center, lax.rsqrt(spread + EPSILON))
            for rows, center, scale in found:
                a[layer, rows, :] = (center * scale * gain).astype(BF16)
                rstd_in[layer, rows, :] = jnp.broadcast_to(scale, (128, 128))

    def hidden(layer, z):
        per_level = ALL_ROWS // levels // WIDTH
        low, high, half = z * per_level, (z + 1) * per_level, HALF // WIDTH

        @pl.loop(jnp.minimum(low, half), jnp.minimum(high, half))
        def _(i):
            cols = row_chunk(i, WIDTH)
            for at in range(0, tokens, PART):
                rows = pl.ds(at, PART)
                value, slope = gelu_and_slope(dot(a[layer, rows, :], weights[layer, cols, :], 1, 1))
                u[rows, cols] = value.astype(BF16)
                gp[rows, cols] = slope

        @pl.loop(jnp.clip(low, half, 2 * half), jnp.clip(high, half, 2 * half))
        def _(i):
            cols_all = row_chunk(i, WIDTH)
            cols = row_chunk(i - half, WIDTH)
            for at in range(0, tokens, PART):
                rows = pl.ds(at, PART)
                z = dot(a[layer, rows, :], weights[layer, cols_all, :], 1, 1)
                value, slope = gelu_and_slope(z)
                vf[rows, cols] = value
                gp[rows, cols_all] = slope
                acc1[rows, :] += lane_groups(value)

    def norm_mid(layer):
        gain = gains[layer : layer + 1, D : D + HALF]
        for r in range(rows_here):
            rows = pl.ds(r * S, S)
            mean = jnp.sum(acc1[rows, :], axis=1, keepdims=True) * (1.0 / HALF)
            acc1[rows, :] = jnp.broadcast_to(mean, (S, 128))

        @pl.loop(0, tokens // 64)
        def _(i):
            rows = row_chunk(i, 64)
            center = vf[rows, :] - lanes(acc1[rows, :], HALF)
            acc2[rows, :] = lane_groups(center * center)

        for r in range(rows_here):
            rows = pl.ds(r * S, S)
            spread = jnp.sum(acc2[rows, :], axis=1, keepdims=True) * (1.0 / HALF)
            rstd_mid[layer, rows, :] = jnp.broadcast_to(lax.rsqrt(spread + EPSILON), (S, 128))

        @pl.loop(0, tokens // 64)
        def _(i):
            rows = row_chunk(i, 64)
            center = vf[rows, :] - lanes(acc1[rows, :], HALF)
            n[rows, :] = (center * lanes(rstd_mid[layer, rows, :], HALF) * gain).astype(BF16)

    def mask_weights(layer):
        spatial = weights[layer, FF + HALF :, :].astype(F32)
        spatial_t = spatial.T
        for r in range(rows_here):
            keep = same(r)
            masked[r] = jnp.where(keep, spatial, 0.0).astype(BF16)
            masked_t[r] = jnp.where(keep, spatial_t, 0.0).astype(BF16)
        line = jnp.broadcast_to(gains[layer : layer + 1, D + HALF :], (128, S))
        bias_t[...] = line.T

    def gated_rows(block, at, size):
        return pl.ds(pl.multiple_of(block * tokens + at, PART), size)

    def mix(layer, hooks=()):
        @pl.loop(0, HALF // BLOCK)
        def _(i):
            between(i, hooks)
            cols = row_chunk(i, BLOCK)
            for r in range(rows_here):
                for at in range(0, S, PART):
                    rows = pl.ds(r * S + at, PART)
                    mixed = dot(masked[r, at : at + PART, :], n[r * S : r * S + S, cols], 1, 0)
                    mixed = mixed + lanes(bias_t[at : at + PART, :], BLOCK)
                    s[rows, cols] = mixed.astype(BF16)
                    gated = (u[rows, cols].astype(F32) * mixed).astype(BF16)
                    grads[0, gated_rows(i, r * S + at, PART), :] = gated

    def project(layer, hooks=()):
        @pl.loop(0, tokens // S)
        def _(i):
            between(i, hooks)
            rows = row_chunk(i, S)
            values = xb[rows, :].astype(F32) if layer == 0 else xf[rows, :]
            for k in range(HALF // BLOCK):
                part = weights[layer, FF + k * BLOCK : FF + (k + 1) * BLOCK, :]
                values = values + dot(grads[0, gated_rows(k, i * S, S), :], part, 1, 0)
            xf[rows, :] = values

    def back_project(layer, hooks=()):
        @pl.loop(0, HALF // BLOCK)
        def _(i):
            between(i, hooks)
            cols = row_chunk(i, BLOCK)
            w_rows = pl.ds(pl.multiple_of(FF + i * BLOCK, BLOCK), BLOCK)
            for at in range(0, tokens, PART):
                rows, here = pl.ds(at, PART), pl.ds(at % S, PART)
                dy = dot(xb[rows, :], weights[layer, w_rows, :], 1, 1).astype(BF16)
                gate, mixed = u[rows, cols], s[rows, cols]
                ds = dy * gate
                u[rows, cols] = gate * mixed
                s[rows, cols] = ds
                gp[rows, cols] = dy * mixed * gp[rows, cols]
                part = lane_groups(ds.astype(F32))
                if at < S:
                    part = part + jnp.where(i == 0, 0.0, bias_sum[here, :])
                else:
                    part = part + bias_sum[here, :]
                bias_sum[here, :] = part
            grads[layer, w_rows, :] = dot(u[:, cols], xb[...], 0, 0).astype(BF16)

    def back_input_weights(layer, low, hooks=(), turn=0):
        count = HALF // BLOCK

        @pl.loop(0, count)
        def _(i):
            between(i, hooks)
            cols = row_chunk(low + lax.rem(i + turn, count), BLOCK)
            grads[layer, cols, :] = dot(gp[:, cols], a[layer], 0, 0).astype(BF16)

    def back_spatial(layer):
        total = None
        for r in range(rows_here):
            rows = pl.ds(r * S, S)
            outer = jnp.where(same(r), dot(s[rows, :], n[rows, :], 1, 1), 0.0)
            total = outer if total is None else total + outer
        grads[layer, FF + HALF :, :] = total.astype(BF16)
        at = layer * VEC + D + HALF
        vec_sum[:, at : at + S] = jnp.sum(bias_sum[...].T, axis=0, keepdims=True)

    def back_mix(layer, hooks=()):
        @pl.loop(0, HALF // BLOCK)
        def _(i):
            between(i, hooks)
            cols = row_chunk(i, BLOCK)
            at_cols = pl.ds(pl.multiple_of(D + i * BLOCK, BLOCK), BLOCK)
            to = pl.ds(pl.multiple_of(layer * VEC + D + i * BLOCK, BLOCK), BLOCK)
            column = jnp.zeros((8, BLOCK), F32)
            for r in range(rows_here):
                for at in range(0, S, PART):
                    rows = pl.ds(r * S + at, PART)
                    dn = dot(masked_t[r, at : at + PART, :], s[r * S : r * S + S, cols], 1, 0)
                    e = dn * gains[layer : layer + 1, at_cols]
                    dn_n = dn * n[rows, cols].astype(F32)
                    vf[rows, cols] = e
                    part_e, part_ew = lane_groups(e), lane_groups(dn_n)
                    acc1[rows, :] = jnp.where(i == 0, part_e, acc1[rows, :] + part_e)
                    acc2[rows, :] = jnp.where(i == 0, part_ew, acc2[rows, :] + part_ew)
                    column = column + jnp.sum(dn_n.reshape(PART // 8, 8, BLOCK), axis=0)
            column = jnp.sum(column, axis=0, keepdims=True)
            vec_sum[:, to] = column * inv_gains[layer : layer + 1, at_cols]

    def back_norm_mid(layer):
        inverse = inv_gains[layer : layer + 1, D : D + HALF]
        for r in range(rows_here):
            rows = pl.ds(r * S, S)
            for acc in (acc1, acc2):
                mean = jnp.sum(acc[rows, :], axis=1, keepdims=True) * (1.0 / HALF)
                acc[rows, :] = jnp.broadcast_to(mean, (S, 128))

        @pl.loop(0, tokens // 64)
        def _(i):
            rows = row_chunk(i, 64)
            mean_e = lanes(acc1[rows, :], HALF)
            mean_ew = lanes(acc2[rows, :], HALF)
            dv = vf[rows, :] - mean_e - n[rows, :].astype(F32) * inverse * mean_ew
            dv = (dv * lanes(rstd_mid[layer, rows, :], HALF)).astype(BF16)
            gp[rows, HALF:] = dv * gp[rows, HALF:]

    def back_input(layer, hooks=()):
        gain = gains[layer : layer + 1, :D]
        inverse = inv_gains[layer : layer + 1, :D]
        at = layer * VEC
        vec_sum[:, at : at + D] = jnp.zeros((1, D), F32)

        @pl.loop(0, tokens // PART)
        def _(i):
            between(i, hooks)
            rows = row_chunk(i, PART)
            da = dot(gp[rows, :], weights[layer, :FF, :], 1, 0)
            normed = a[layer, rows, :].astype(F32)
            product = da * normed
            e = da * gain
            mean_e = jnp.sum(lane_groups(e), axis=1, keepdims=True) * (1.0 / D)
            mean_ew = jnp.sum(lane_groups(product), axis=1, keepdims=True) * (1.0 / D)
            dx = (e - mean_e - normed * inverse * mean_ew) * lanes(rstd_in[layer, rows, :], D)
            above = xb[rows, :].astype(F32) if layer == LAYERS - 1 else xf[rows, :]
            total = above + dx
            xf[rows, :] = total
            if layer:
                xb[rows, :] = total.astype(BF16)
            vec_sum[:, at : at + D] += jnp.sum(product, axis=0, keepdims=True) * inverse

    def later(act, *where):
        return (lambda: act(*where)) if linked else None

    def norm_mid_early(layer, early):
        if linked:
            pl.when(not_top if early else jnp.logical_not(not_top))(lambda: norm_mid(layer))
        elif not early:
            norm_mid(layer)

    def take(layer, step):
        if linked:
            gather_twin(layer, step)
        hidden(layer, sources[step] if linked else step)

    if linked:
        gather_depart(0)
        gather_line(0, 0)
        prepare()
        load_tok.wait()
        norm_in(0)
        gather_line(0, 1)
        gather_first(0, 0)
        gather_line(0, 2)
        gather_first(0, 1)
        gather_second(0, 0)
        take(0, 0)
        gather_first(0, 2)
        gather_second(0, 1)
        gather_line(0, 3)
        gather_depart(1)
        take(0, 1)
        gather_second(0, 2)
        gather_first(0, 3)
        gather_line(1, 0)
        take(0, 2)
        gather_second(0, 3)
        gather_line(1, 1)
        gather_first(1, 0)
    else:
        prepare()
        for copy in load_mats:
            copy.wait()
        load_tok.wait()
        norm_in(0)
        for step in range(levels - 1):
            take(0, step)
    norm_mid_early(0, True)
    take(0, levels - 1)
    norm_mid_early(0, False)
    keep_u = pltpu.make_async_copy(u, park_u, local_sem.at[3])
    keep_u.start()
    keep_g = pltpu.make_async_copy(gp, park_g, local_sem.at[4])
    keep_g.start()
    keep_n = pltpu.make_async_copy(n, park_n, local_sem.at[5])
    keep_n.start()
    mask_weights(0)
    mix(0, (later(gather_line, 1, 2), later(gather_first, 1, 1), None))
    keep_s = pltpu.make_async_copy(s, park_s, local_sem.at[6])
    keep_s.start()
    project(0, (None, later(gather_second, 1, 0)))
    load_cot = pltpu.make_async_copy(cot, xb, local_sem.at[0])
    load_cot.start()
    norm_in(1)
    acc1[...] = jnp.zeros_like(acc1)
    keep_u.wait()
    keep_g.wait()
    for step in range(levels - 1):
        take(1, step)
        if linked:
            if step < 2:
                gather_first(1, step + 2)
            gather_second(1, step + 1)
            if step == 0:
                gather_line(1, 3)
    keep_n.wait()
    norm_mid_early(1, True)
    take(1, levels - 1)
    norm_mid_early(1, False)
    mask_weights(1)
    keep_s.wait()
    mix(1)
    load_cot.wait()

    back_project(1)
    back_input_weights(1, 0)
    load_u = pltpu.make_async_copy(park_u, u, local_sem.at[3])
    load_u.start()
    if linked:
        reduce_begin(1, 0)
    project(1)
    write_out = pltpu.make_async_copy(xf, out, local_sem.at[1])
    write_out.start()
    if linked:
        reduce_second(1, 0)
    back_spatial(1)
    if linked:
        reduce_begin(1, 3)
    back_mix(1, (None, later(reduce_second, 1, 3), None))
    load_s = pltpu.make_async_copy(park_s, s, local_sem.at[6])
    load_s.start()
    back_norm_mid(1)
    load_n = pltpu.make_async_copy(park_n, n, local_sem.at[5])
    load_n.start()
    if linked:
        reduce_first(1, 0)
    half = HALF // BLOCK
    back_input_weights(1, half, (None, later(reduce_begin, 1, 2), later(reduce_second, 1, 2)), 2)
    if linked:
        reduce_begin(1, 1)
        reduce_first(1, 3)
    write_out.wait()
    back_input(1, (later(reduce_second, 1, 1), None, later(reduce_line, 1, 0), None))
    load_g = pltpu.make_async_copy(park_g, gp, local_sem.at[4])
    load_g.start()
    if linked:
        gather_sent(1)
        for device in links.partners():
            pl.semaphore_signal(credit, inc=1, device_id=device, device_id_type=MESH)
        reduce_first(1, 2)

    mask_weights(0)
    load_u.wait()
    load_s.wait()
    load_g.wait()
    back_project(0, (None, later(reduce_line, 1, 3), None))
    back_input_weights(0, 0, (later(reduce_first, 1, 1), None, later(reduce_line, 1, 2)))
    if linked:
        pl.semaphore_wait(credit, len(links.partners()))
        reduce_begin(0, 0)
    load_n.wait()
    back_spatial(0)
    if linked:
        reduce_second(0, 0)
        reduce_begin(0, 3)
    back_mix(0, (None, later(reduce_second, 0, 3), later(reduce_line, 1, 1)))
    back_norm_mid(0)
    if linked:
        reduce_first(0, 0)
    back_input_weights(0, half, (None, later(reduce_begin, 0, 2), later(reduce_second, 0, 2)), 2)
    if linked:
        reduce_begin(0, 1)
        reduce_first(0, 3)
        reduce_end(1)
    back_input(0, (later(reduce_second, 0, 1), None, later(reduce_line, 0, 0), None))
    write_in = pltpu.make_async_copy(xf, grad_in, local_sem.at[0])
    write_in.start()
    if linked:
        vec_pair(0, links.twin).start()
        reduce_first(0, 2)
        vec_add(0, links.twin)
        vec_pair(1, links.along_y).start()
        reduce_line(0, 3)
        vec_add(1, links.along_y)
        vec_pair(2, links.along_x).start()
        reduce_first(0, 1)
        vec_add(2, links.along_x)
        vec_line_begin()
        reduce_line(0, 2)
        reduce_line(0, 1)
        total = vec_line_end()
        reduce_end(0)
        gather_sent(0)
        for where in started:
            reduce_copy(*where).wait_send()
        for layer in range(LAYERS):
            mat_copy(layer).wait()
    else:
        total = vec_sum[...]
        for layer in range(LAYERS):
            copy = pltpu.make_async_copy(grads.at[layer], mat_out.at[layer], local_sem.at[1])
            copy.start()
            copy.wait()
    for layer in range(LAYERS):
        vec_out[layer : layer + 1, :] = total[:, layer * VEC : (layer + 1) * VEC]
    write_in.wait()


def per_device(wide, narrow, tokens, segment_ids, matrices, vectors, cotangent):
    axes = ("wide", "narrow")
    count, share = tokens.shape[0], matrices.shape[1]
    total = count * S
    linked = narrow == 4 and wide == 8 and share % 16 == 0
    if not linked:
        matrices = lax.all_gather(matrices, axes, axis=1, tiled=True)
    levels = wide // 2 if linked else 4
    anywhere = pl.BlockSpec(memory_space=pl.ANY)
    vmem = pl.BlockSpec(memory_space=pltpu.VMEM)
    mat_shape = (LAYERS, share, D) if linked else (LAYERS, ALL_ROWS, D)
    half, full = (total, HALF), (total, FF)
    dma = pltpu.SemaphoreType.DMA
    flags = dict(collective_id=0) if linked else {}
    results = pl.pallas_call(
        functools.partial(kernel, wide, narrow, linked),
        out_shape=(
            jax.ShapeDtypeStruct((total, D), F32),
            jax.ShapeDtypeStruct((total, D), F32),
            jax.ShapeDtypeStruct(mat_shape, F32 if linked else BF16),
            jax.ShapeDtypeStruct((LAYERS, VEC), F32),
            jax.ShapeDtypeStruct(half, BF16),
            jax.ShapeDtypeStruct(half, BF16),
            jax.ShapeDtypeStruct(half, BF16),
            jax.ShapeDtypeStruct(full, BF16),
        ),
        in_specs=[anywhere, vmem, anywhere, vmem, anywhere],
        out_specs=(anywhere, anywhere, anywhere, vmem) + (anywhere,) * 4,
        scratch_shapes=[
            pltpu.VMEM((LAYERS, ALL_ROWS, D), BF16),
            pltpu.VMEM((LAYERS, ALL_ROWS, D), BF16),
            pltpu.VMEM((ALL_ROWS if linked else 16, D), BF16),
            pltpu.VMEM(half, BF16),
            pltpu.VMEM(full, BF16),
            pltpu.VMEM(half, BF16),
            pltpu.VMEM(half, BF16),
            pltpu.VMEM((LAYERS, total, D), BF16),
            pltpu.VMEM((total, D), F32),
            pltpu.VMEM((total, D), BF16),
            pltpu.VMEM((count, S, S), BF16),
            pltpu.VMEM((count, S, S), BF16),
            pltpu.VMEM((LAYERS, total, 128), F32),
            pltpu.VMEM((LAYERS, total, 128), F32),
            pltpu.VMEM((total, 128), F32),
            pltpu.VMEM((total, 128), F32),
            pltpu.VMEM((total, HALF), F32),
            pltpu.VMEM((LAYERS, share if linked else 8, D), F32),
            pltpu.VMEM((count, S, 128), F32),
            pltpu.VMEM((S, 128), F32),
            pltpu.VMEM((S, 128), F32),
            pltpu.VMEM((LAYERS, VEC), F32),
            pltpu.VMEM((LAYERS, VEC), F32),
            pltpu.VMEM((1, LAYERS * VEC), F32),
            pltpu.VMEM((levels + 3, 1, LAYERS * VEC), F32),
            dma((7,)),
            pltpu.SemaphoreType.REGULAR,
            dma((LAYERS, levels, 7 + levels)),
            dma((LAYERS, levels, 8)),
            dma((LAYERS, levels, 8)),
            dma((LAYERS, levels, 8)),
            dma((levels + 3,)),
            dma((levels + 3,)),
        ],
        compiler_params=pltpu.CompilerParams(
            has_side_effects=True, vmem_limit_bytes=63 << 20, **flags
        ),
    )(
        tokens.reshape(total, D),
        segment_ids,
        matrices,
        vectors,
        cotangent.reshape(total, D),
    )
    out, grad_in, mat_grads, vec_grads = results[:4]
    if not linked:
        mat_grads = lax.psum_scatter(
            mat_grads.astype(F32), axes, scatter_dimension=1, tiled=True
        )
        vec_grads = lax.psum(vec_grads, axes)
    return (out.reshape(tokens.shape), grad_in.reshape(tokens.shape), mat_grads, vec_grads)


def solution(mesh):
    rows = P(("wide", "narrow"), None, None)
    spread = P(None, ("wide", "narrow"), None)
    return jax.shard_map(
        functools.partial(per_device, mesh.shape["wide"], mesh.shape["narrow"]),
        mesh=mesh,
        in_specs=(rows, P(("wide", "narrow"), None), spread, P(), rows),
        out_specs=(rows, rows, spread, P()),
        check_vma=False,
    )
```

```python
import functools

import jax
import jax.numpy as jnp
from jax import lax
from jax.experimental import pallas as pl
from jax.experimental.pallas import tpu as pltpu
from jax.sharding import PartitionSpec as P

D = 512
FF = 3072
HALF = FF // 2
S = 512
LAYERS = 2
VEC = D + HALF + S
ALL_ROWS = FF + HALF + S
EPSILON = 1e-05
BLOCK = 512
PART = 256
WIDTH = 256
MESH = pl.DeviceIdType.MESH
BF16 = jnp.bfloat16
F32 = jnp.float32
GELU_A = 0.7978845608028654
GELU_B = 0.044715


def dot(left, right, left_dim, right_dim):
    dims = (((left_dim,), (right_dim,)), ((), ()))
    return lax.dot_general(left, right, dims, preferred_element_type=F32)


def gelu_and_slope(z):
    squared = z * z
    share = 0.5 + 0.5 * jnp.tanh(z * (GELU_A + (GELU_A * GELU_B) * squared))
    value = z * share
    near, gate = value.astype(BF16), share.astype(BF16)
    rise = BF16(2.0 * GELU_A) + BF16(6.0 * GELU_A * GELU_B) * squared.astype(BF16)
    return value, gate + (near - near * gate) * rise


def lane_groups(values):
    total = values[:, :128]
    for at in range(128, values.shape[1], 128):
        total = total + values[:, at : at + 128]
    return total


def lanes(column, width):
    return jnp.concatenate([column] * (width // 128), axis=1)


class Links:
    def __init__(self, wide, narrow, share):
        self.share = share
        self.levels = wide // 2
        self.narrow = narrow
        self.w = lax.axis_index("wide")
        self.n = lax.axis_index("narrow")
        self.x = self.w % 2
        self.z = self.w // 2
        self.core = self.n % 2
        self.y = self.n // 2
        other_w = self.w + 1 - 2 * self.x
        other_n = self.n + 2 - 4 * self.y
        self.first = self.mix((other_w, self.n), (self.w, other_n))
        self.second = self.mix((self.w, other_n), (other_w, self.n))
        self.twin = (self.w, self.n + 1 - 2 * self.core)
        self.along_x = (other_w, self.n)
        self.along_y = (self.w, other_n)

    def mix(self, zero, one):
        return tuple((1 - self.core) * a + self.core * b for a, b in zip(zero, one))

    def line(self, z):
        return (2 * z + self.x, self.n)

    def partners(self):
        found = [self.twin, self.first, self.second]
        for step in range(1, self.levels):
            found.append(self.line((self.z + step) % self.levels))
        return found

    def rows(self, w, n):
        return pl.ds(pl.multiple_of((w * self.narrow + n) * self.share, 16), self.share)

    def shards(self, z):
        out = []
        for n, n_first, n_second, w_first, w_second in (
            (self.n, self.first[1], self.second[1], self.first[0], self.second[0]),
            (
                self.twin[1],
                self.twin[1] + (1 - self.core) * (2 - 4 * self.y),
                self.twin[1] + self.core * (2 - 4 * self.y),
                self.w + self.core * (1 - 2 * self.x),
                self.w + (1 - self.core) * (1 - 2 * self.x),
            ),
        ):
            cross = n + 2 - 4 * self.y
            out.append(self.rows(2 * z + self.x, n))
            out.append(self.rows(2 * z + w_first % 2, n_first))
            out.append(self.rows(2 * z + w_second % 2, n_second))
            out.append(self.rows(2 * z + 1 - self.x, cross))
        return out


def send(source, target, send_sem, recv_sem, device):
    return pltpu.make_async_remote_copy(
        src_ref=source,
        dst_ref=target,
        send_sem=send_sem,
        recv_sem=recv_sem,
        device_id=device,
        device_id_type=MESH,
    )


def kernel(wide, narrow, linked, tok, seg, mats, vec, cot, *refs):
    out, grad_in, mat_out, vec_out, park_u, park_s, park_n, park_g = refs[:8]
    (
        weights,
        grads,
        landing,
        u,
        gp,
        s,
        n,
        a,
        xf,
        xb,
        masked,
        masked_t,
        rstd_in,
        rstd_mid,
        acc1,
        acc2,
        vf,
        mat_stage,
        seg_t,
        bias_t,
        bias_sum,
        gains,
        inv_gains,
        vec_sum,
        vec_in,
        local_sem,
        credit,
        g_send,
        g_recv,
        r_send,
        r_recv,
        v_send,
        v_recv,
    ) = refs[8:]
    tokens = xf.shape[0]
    rows_here = tokens // S
    share = mats.shape[1]
    links = Links(wide, narrow, share) if linked else None
    levels = wide // 2 if linked else 4
    passed_on, started = ([], []), []

    load_tok = pltpu.make_async_copy(tok, xb, local_sem.at[0])
    load_tok.start()
    load_mats = []
    for layer in range(LAYERS):
        place = links.rows(links.w, links.n) if linked else pl.ds(0, ALL_ROWS)
        copy = pltpu.make_async_copy(
            mats.at[layer], weights.at[layer, place], local_sem.at[1 + layer]
        )
        copy.start()
        load_mats.append(copy)

    if linked:
        barrier = pltpu.get_barrier_semaphore()
        for device in links.partners():
            pl.semaphore_signal(barrier, inc=1, device_id=device, device_id_type=MESH)
        pl.semaphore_wait(barrier, len(links.partners()))

    if linked:
        sources, targets = [], []
        for step in range(levels):
            below = (links.z - step + 2 * levels) // (2 * levels)
            sources.append(below * (links.z - step) + (1 - below) * step)
        for step in range(1, levels):
            above = (levels - 1 - links.z - step + 2 * levels) // (2 * levels)
            upward = links.z + step
            downward = levels - 1 - step
            targets.append(links.line(above * upward + (1 - above) * downward))
        not_top = links.z < levels - 1
        shards_of = [links.shards(z) for z in sources]

    def gather_copy(layer, step, slot, send_slot, target_slot, device):
        rows = shards_of[step][slot]
        return send(
            weights.at[layer, rows],
            weights.at[layer, rows],
            g_send.at[layer, sources[step], send_slot],
            g_recv.at[layer, sources[step], target_slot],
            device,
        )

    def pass_on(layer, step, slot, send_slot, target_slot, device):
        again = functools.partial(gather_copy, layer, step, slot, send_slot, target_slot, device)
        again().start()
        passed_on[layer].append(again)

    def arrived(layer, step, slot):
        gather_copy(layer, step, slot, 0, slot, links.twin).wait_recv()

    def gather_depart(layer):
        load_mats[layer].wait()
        for at, device in enumerate(targets):
            pass_on(layer, 0, 0, 7 + at, 0, device)

    def gather_line(layer, step):
        if step:
            arrived(layer, step, 0)
        pass_on(layer, step, 0, 0, 1, links.first)
        pass_on(layer, step, 0, 1, 2, links.second)
        pass_on(layer, step, 0, 3, 4, links.twin)

    def gather_first(layer, step):
        arrived(layer, step, 1)
        pass_on(layer, step, 1, 2, 3, links.second)
        pass_on(layer, step, 1, 4, 5, links.twin)

    def gather_second(layer, step):
        for slot in (2, 3):
            arrived(layer, step, slot)
            pass_on(layer, step, slot, 3 + slot, 4 + slot, links.twin)

    def gather_twin(layer, step):
        for slot in range(4, 8):
            arrived(layer, step, slot)

    def gather_sent(layer):
        for again in passed_on[layer]:
            again().wait_send()

    if linked:
        shards_at = [links.shards(z) for z in range(levels)]
        own_shards = links.shards(links.z)

    def land(layer, index):
        rows = pl.ds(pl.multiple_of(index * share, 16), share)
        return weights.at[1, rows] if layer == 0 else landing.at[rows]

    def add_in(layer, rows, index):
        grads[layer, rows, :] = (
            grads[layer, rows, :].astype(F32) + land(layer, index)[...].astype(F32)
        ).astype(BF16)

    def reduce_copy(layer, z, rows, target, slot, device, recv_z=None):
        return send(
            grads.at[layer, rows],
            land(layer, target),
            r_send.at[layer, z, slot],
            r_recv.at[layer, z if recv_z is None else recv_z, slot],
            device,
        )

    def reduce_start(*where):
        reduce_copy(*where).start()
        started.append(where)

    def reduce_sent(layer):
        for where in started:
            if where[0] == layer:
                reduce_copy(*where).wait_send()

    def reduce_begin(layer, z):
        shards = shards_at[z]
        for slot in range(4):
            reduce_start(layer, z, shards[4 + slot], 4 * z + slot, slot, links.twin)

    def reduce_second(layer, z):
        shards = shards_at[z]
        for slot in (2, 3, 0, 1):
            reduce_copy(layer, z, shards[slot], 4 * z + slot, slot, links.twin).wait_recv()
            add_in(layer, shards[slot], 4 * z + slot)
            if slot >= 2:
                index = 4 * levels + 2 * z + slot - 2
                reduce_start(layer, z, shards[slot], index, 2 + slot, links.second)

    def reduce_first(layer, z):
        shards = shards_at[z]
        for slot in (1, 0):
            index = 4 * levels + 2 * z + slot
            reduce_copy(layer, z, shards[slot], index, 4 + slot, links.second).wait_recv()
            add_in(layer, shards[slot], index)
            if slot == 1:
                reduce_start(layer, z, shards[1], 6 * levels + z, 6, links.first)

    def line_copy(layer, z):
        return reduce_copy(
            layer, z, shards_at[z][0], 7 * levels + links.z, 7, links.line(z), links.z
        )

    def reduce_line(layer, z):
        shards = shards_at[z]
        index = 6 * levels + z
        reduce_copy(layer, z, shards[0], index, 6, links.first).wait_recv()
        add_in(layer, shards[0], index)

        @pl.when(links.z != z)
        def _():
            line_copy(layer, z).start()

    def mat_copy(layer):
        return pltpu.make_async_copy(mat_stage.at[layer], mat_out.at[layer], local_sem.at[1 + layer])

    def reduce_end(layer):
        shards = own_shards
        total = grads[layer, shards[0], :].astype(F32)
        for step in range(1, levels):
            z = (links.z + step) % levels
            reduce_copy(layer, z, shards[0], 7 * levels + z, 7, links.line(z)).wait_recv()
            total = total + land(layer, 7 * levels + z)[...].astype(F32)
        mat_stage[layer] = total
        mat_copy(layer).start()
        for z in range(levels):

            @pl.when(links.z != z)
            def _():
                line_copy(layer, z).wait_send()

    def vec_pair(index, device):
        return send(vec_sum, vec_in.at[levels + index], v_send.at[index], v_recv.at[index], device)

    def vec_add(index, device):
        vec_pair(index, device).wait()
        vec_sum[...] = vec_sum[...] + vec_in[levels + index]

    def vec_copy(step, z):
        return send(
            vec_sum,
            vec_in.at[z],
            v_send.at[2 + step],
            v_recv.at[3 + z],
            links.line((links.z + step) % levels),
        )

    def vec_line_begin():
        for step in range(1, levels):
            vec_copy(step, links.z).start()

    def vec_line_end():
        for step in range(1, levels):
            vec_copy(step, (links.z + step) % levels).wait_recv()
        for step in range(1, levels):
            vec_copy(step, links.z).wait_send()
        vec_in[pl.ds(links.z, 1)] = vec_sum[...][None]
        total = vec_in[0]
        for z in range(1, levels):
            total = total + vec_in[z]
        return total

    def prepare():
        gains[...] = vec[...].astype(F32)
        inv_gains[...] = 1.0 / gains[...]
        for r in range(rows_here):
            line = jnp.broadcast_to(seg[r : r + 1, :].astype(F32), (128, S))
            seg_t[r] = line.T
        acc1[...] = jnp.zeros_like(acc1)

    def same(r):
        return lanes(seg_t[r], S) == seg[r : r + 1, :].astype(F32)

    def row_chunk(i, size):
        return pl.ds(pl.multiple_of(i * size, size), size)

    def between(i, hooks):
        for at, hook in enumerate(hooks):
            if hook is not None:
                pl.when(i == at)(hook)

    def norm_in(layer):
        gain = gains[layer : layer + 1, :D]

        @pl.loop(0, tokens // 256)
        def _(i):
            found = []
            for part in range(2):
                rows = row_chunk(2 * i + part, 128)
                values = xb[rows, :].astype(F32) if layer == 0 else xf[rows, :]
                mean = jnp.sum(lane_groups(values), axis=1, keepdims=True) * (1.0 / D)
                found.append((rows, values - mean))
            for at, (rows, center) in enumerate(found):
                spread = jnp.sum(lane_groups(center * center), axis=1, keepdims=True) * (1.0 / D)
                found[at] = (rows, center, lax.rsqrt(spread + EPSILON))
            for rows, center, scale in found:
                a[layer, rows, :] = (center * scale * gain).astype(BF16)
                rstd_in[layer, rows, :] = jnp.broadcast_to(scale, (128, 128))

    def hidden(layer, z):
        per_level = ALL_ROWS // levels // WIDTH
        low, high, half = z * per_level, (z + 1) * per_level, HALF // WIDTH

        @pl.loop(jnp.minimum(low, half), jnp.minimum(high, half))
        def _(i):
            cols = row_chunk(i, WIDTH)
            for at in range(0, tokens, PART):
                rows = pl.ds(at, PART)
                value, slope = gelu_and_slope(dot(a[layer, rows, :], weights[layer, cols, :], 1, 1))
                u[rows, cols] = value.astype(BF16)
                gp[rows, cols] = slope

        @pl.loop(jnp.clip(low, half, 2 * half), jnp.clip(high, half, 2 * half))
        def _(i):
            cols_all = row_chunk(i, WIDTH)
            cols = row_chunk(i - half, WIDTH)
            for at in range(0, tokens, PART):
                rows = pl.ds(at, PART)
                z = dot(a[layer, rows, :], weights[layer, cols_all, :], 1, 1)
                value, slope = gelu_and_slope(z)
                vf[rows, cols] = value
                gp[rows, cols_all] = slope
                acc1[rows, :] += lane_groups(value)

    def norm_mid(layer):
        gain = gains[layer : layer + 1, D : D + HALF]
        for r in range(rows_here):
            rows = pl.ds(r * S, S)
            mean = jnp.sum(acc1[rows, :], axis=1, keepdims=True) * (1.0 / HALF)
            acc1[rows, :] = jnp.broadcast_to(mean, (S, 128))

        @pl.loop(0, tokens // 64)
        def _(i):
            rows = row_chunk(i, 64)
            center = vf[rows, :] - lanes(acc1[rows, :], HALF)
            acc2[rows, :] = lane_groups(center * center)

        for r in range(rows_here):
            rows = pl.ds(r * S, S)
            spread = jnp.sum(acc2[rows, :], axis=1, keepdims=True) * (1.0 / HALF)
            rstd_mid[layer, rows, :] = jnp.broadcast_to(lax.rsqrt(spread + EPSILON), (S, 128))

        @pl.loop(0, tokens // 64)
        def _(i):
            rows = row_chunk(i, 64)
            center = vf[rows, :] - lanes(acc1[rows, :], HALF)
            n[rows, :] = (center * lanes(rstd_mid[layer, rows, :], HALF) * gain).astype(BF16)

    def mask_weights(layer):
        spatial = weights[layer, FF + HALF :, :].astype(F32)
        spatial_t = spatial.T
        for r in range(rows_here):
            keep = same(r)
            masked[r] = jnp.where(keep, spatial, 0.0).astype(BF16)
            masked_t[r] = jnp.where(keep, spatial_t, 0.0).astype(BF16)
        line = jnp.broadcast_to(gains[layer : layer + 1, D + HALF :], (128, S))
        bias_t[...] = line.T

    def gated_rows(block, at, size):
        return pl.ds(pl.multiple_of(block * tokens + at, PART), size)

    def mix(layer, hooks=()):
        @pl.loop(0, HALF // BLOCK)
        def _(i):
            between(i, hooks)
            cols = row_chunk(i, BLOCK)
            for r in range(rows_here):
                for at in range(0, S, PART):
                    rows = pl.ds(r * S + at, PART)
                    mixed = dot(masked[r, at : at + PART, :], n[r * S : r * S + S, cols], 1, 0)
                    mixed = mixed + lanes(bias_t[at : at + PART, :], BLOCK)
                    s[rows, cols] = mixed.astype(BF16)
                    gated = (u[rows, cols].astype(F32) * mixed).astype(BF16)
                    grads[0, gated_rows(i, r * S + at, PART), :] = gated

    def project(layer, hooks=()):
        @pl.loop(0, tokens // S)
        def _(i):
            between(i, hooks)
            rows = row_chunk(i, S)
            values = xb[rows, :].astype(F32) if layer == 0 else xf[rows, :]
            for k in range(HALF // BLOCK):
                part = weights[layer, FF + k * BLOCK : FF + (k + 1) * BLOCK, :]
                values = values + dot(grads[0, gated_rows(k, i * S, S), :], part, 1, 0)
            xf[rows, :] = values

    def back_project(layer, hooks=(), weights_too=True):
        @pl.loop(0, HALF // BLOCK)
        def _(i):
            between(i, hooks)
            cols = row_chunk(i, BLOCK)
            w_rows = pl.ds(pl.multiple_of(FF + i * BLOCK, BLOCK), BLOCK)
            for at in range(0, tokens, PART):
                rows, here = pl.ds(at, PART), pl.ds(at % S, PART)
                dy = dot(xb[rows, :], weights[layer, w_rows, :], 1, 1).astype(BF16)
                gate, mixed = u[rows, cols], s[rows, cols]
                ds = dy * gate
                u[rows, cols] = gate * mixed
                s[rows, cols] = ds
                gp[rows, cols] = dy * mixed * gp[rows, cols]
                part = lane_groups(ds.astype(F32))
                if at < S:
                    part = part + jnp.where(i == 0, 0.0, bias_sum[here, :])
                else:
                    part = part + bias_sum[here, :]
                bias_sum[here, :] = part
            if weights_too:
                grads[layer, w_rows, :] = dot(u[:, cols], xb[...], 0, 0).astype(BF16)

    def back_output_weights(layer):
        @pl.loop(0, HALF // BLOCK)
        def _(i):
            w_rows = pl.ds(pl.multiple_of(FF + i * BLOCK, BLOCK), BLOCK)
            grads[layer, w_rows, :] = dot(u[:, row_chunk(i, BLOCK)], xb[...], 0, 0).astype(BF16)

    def back_input_weights(layer, low, hooks=(), turn=0):
        count = HALF // BLOCK

        @pl.loop(0, count)
        def _(i):
            between(i, hooks)
            cols = row_chunk(low + lax.rem(i + turn, count), BLOCK)
            grads[layer, cols, :] = dot(gp[:, cols], a[layer], 0, 0).astype(BF16)

    def back_spatial(layer):
        total = None
        for r in range(rows_here):
            rows = pl.ds(r * S, S)
            outer = jnp.where(same(r), dot(s[rows, :], n[rows, :], 1, 1), 0.0)
            total = outer if total is None else total + outer
        grads[layer, FF + HALF :, :] = total.astype(BF16)
        at = layer * VEC + D + HALF
        vec_sum[:, at : at + S] = jnp.sum(bias_sum[...].T, axis=0, keepdims=True)

    def back_mix(layer, hooks=()):
        @pl.loop(0, HALF // BLOCK)
        def _(i):
            between(i, hooks)
            cols = row_chunk(i, BLOCK)
            at_cols = pl.ds(pl.multiple_of(D + i * BLOCK, BLOCK), BLOCK)
            to = pl.ds(pl.multiple_of(layer * VEC + D + i * BLOCK, BLOCK), BLOCK)
            column = jnp.zeros((8, BLOCK), F32)
            for r in range(rows_here):
                for at in range(0, S, PART):
                    rows = pl.ds(r * S + at, PART)
                    dn = dot(masked_t[r, at : at + PART, :], s[r * S : r * S + S, cols], 1, 0)
                    e = dn * gains[layer : layer + 1, at_cols]
                    dn_n = dn * n[rows, cols].astype(F32)
                    vf[rows, cols] = e
                    part_e, part_ew = lane_groups(e), lane_groups(dn_n)
                    acc1[rows, :] = jnp.where(i == 0, part_e, acc1[rows, :] + part_e)
                    acc2[rows, :] = jnp.where(i == 0, part_ew, acc2[rows, :] + part_ew)
                    column = column + jnp.sum(dn_n.reshape(PART // 8, 8, BLOCK), axis=0)
            column = jnp.sum(column, axis=0, keepdims=True)
            vec_sum[:, to] = column * inv_gains[layer : layer + 1, at_cols]

    def back_norm_mid(layer):
        inverse = inv_gains[layer : layer + 1, D : D + HALF]
        for r in range(rows_here):
            rows = pl.ds(r * S, S)
            for acc in (acc1, acc2):
                mean = jnp.sum(acc[rows, :], axis=1, keepdims=True) * (1.0 / HALF)
                acc[rows, :] = jnp.broadcast_to(mean, (S, 128))

        @pl.loop(0, tokens // 64)
        def _(i):
            rows = row_chunk(i, 64)
            mean_e = lanes(acc1[rows, :], HALF)
            mean_ew = lanes(acc2[rows, :], HALF)
            dv = vf[rows, :] - mean_e - n[rows, :].astype(F32) * inverse * mean_ew
            dv = (dv * lanes(rstd_mid[layer, rows, :], HALF)).astype(BF16)
            gp[rows, HALF:] = dv * gp[rows, HALF:]

    def back_input(layer, hooks=()):
        gain = gains[layer : layer + 1, :D]
        inverse = inv_gains[layer : layer + 1, :D]
        at = layer * VEC
        vec_sum[:, at : at + D] = jnp.zeros((1, D), F32)

        @pl.loop(0, tokens // PART)
        def _(i):
            between(i, hooks)
            rows = row_chunk(i, PART)
            da = dot(gp[rows, :], weights[layer, :FF, :], 1, 0)
            normed = a[layer, rows, :].astype(F32)
            product = da * normed
            e = da * gain
            mean_e = jnp.sum(lane_groups(e), axis=1, keepdims=True) * (1.0 / D)
            mean_ew = jnp.sum(lane_groups(product), axis=1, keepdims=True) * (1.0 / D)
            dx = (e - mean_e - normed * inverse * mean_ew) * lanes(rstd_in[layer, rows, :], D)
            above = xb[rows, :].astype(F32) if layer == LAYERS - 1 else xf[rows, :]
            total = above + dx
            xf[rows, :] = total
            if layer:
                xb[rows, :] = total.astype(BF16)
            vec_sum[:, at : at + D] += jnp.sum(product, axis=0, keepdims=True) * inverse

    def later(act, *where):
        return (lambda: act(*where)) if linked else None

    def levels_in_turn(layer, after):
        last = levels - 2 + links.z // (levels - 1) if linked else levels - 1

        @pl.loop(0, levels)
        def _(step):
            if linked:
                between(step, [functools.partial(gather_twin, layer, k) for k in range(levels)])
                below = (links.z - step + 2 * levels) // (2 * levels)
                hidden(layer, below * (links.z - step) + (1 - below) * step)
                between(step, after)
            else:
                hidden(layer, step)
            pl.when(step == last)(lambda: norm_mid(layer))

    if linked:
        gather_depart(0)
        gather_line(0, 0)
        prepare()
        load_tok.wait()
        norm_in(0)
        gather_line(0, 1)
        gather_first(0, 0)
        gather_line(0, 2)
        gather_first(0, 1)
        gather_second(0, 0)
    else:
        prepare()
        for copy in load_mats:
            copy.wait()
        load_tok.wait()
        norm_in(0)

    def after_first():
        gather_first(0, 2)
        gather_second(0, 1)
        gather_line(0, 3)
        gather_depart(1)

    def after_second():
        gather_second(0, 2)
        gather_first(0, 3)
        gather_line(1, 0)

    def after_third():
        gather_second(0, 3)
        gather_line(1, 1)
        gather_first(1, 0)

    levels_in_turn(0, (after_first, after_second, after_third))
    keep_u = pltpu.make_async_copy(u, park_u, local_sem.at[3])
    keep_u.start()
    keep_g = pltpu.make_async_copy(gp, park_g, local_sem.at[4])
    keep_g.start()
    keep_n = pltpu.make_async_copy(n, park_n, local_sem.at[5])
    keep_n.start()
    mask_weights(0)
    mix(0, (later(gather_line, 1, 2), later(gather_first, 1, 1), None))
    keep_s = pltpu.make_async_copy(s, park_s, local_sem.at[6])
    keep_s.start()
    project(0, (None, later(gather_second, 1, 0)))
    load_cot = pltpu.make_async_copy(cot, xb, local_sem.at[0])
    load_cot.start()
    norm_in(1)
    acc1[...] = jnp.zeros_like(acc1)
    keep_u.wait()
    keep_g.wait()
    keep_n.wait()

    def after_first_again():
        gather_first(1, 2)
        gather_second(1, 1)
        gather_line(1, 3)

    def after_second_again():
        gather_first(1, 3)
        gather_second(1, 2)

    def after_third_again():
        gather_second(1, 3)

    if linked:
        gather_sent(0)
    levels_in_turn(1, (after_first_again, after_second_again, after_third_again))
    mask_weights(1)
    keep_s.wait()
    mix(1)
    load_cot.wait()

    back_project(1, weights_too=False)
    back_input_weights(1, 0)
    if linked:
        reduce_begin(1, 0)
    back_output_weights(1)
    load_u = pltpu.make_async_copy(park_u, u, local_sem.at[3])
    load_u.start()
    if linked:
        reduce_second(1, 0)
    back_spatial(1)
    if linked:
        reduce_begin(1, 3)
    project(1)
    write_out = pltpu.make_async_copy(xf, out, local_sem.at[1])
    write_out.start()
    if linked:
        reduce_second(1, 3)
    back_mix(1)
    load_s = pltpu.make_async_copy(park_s, s, local_sem.at[6])
    load_s.start()
    back_norm_mid(1)
    load_n = pltpu.make_async_copy(park_n, n, local_sem.at[5])
    load_n.start()
    if linked:
        reduce_first(1, 0)
    half = HALF // BLOCK
    back_input_weights(1, half, (None, later(reduce_begin, 1, 2), later(reduce_second, 1, 2)), 2)
    if linked:
        reduce_begin(1, 1)
        reduce_first(1, 3)
    write_out.wait()
    back_input(1, (later(reduce_second, 1, 1), None, later(reduce_line, 1, 0), None))
    load_g = pltpu.make_async_copy(park_g, gp, local_sem.at[4])
    load_g.start()
    if linked:
        gather_sent(1)
        for device in links.partners():
            pl.semaphore_signal(credit, inc=1, device_id=device, device_id_type=MESH)
        reduce_first(1, 2)

    mask_weights(0)
    load_u.wait()
    load_s.wait()
    load_g.wait()
    back_project(0, (None, later(reduce_line, 1, 3), None))
    back_input_weights(0, 0, (later(reduce_first, 1, 1), None, later(reduce_line, 1, 2)))
    if linked:
        pl.semaphore_wait(credit, len(links.partners()))
        reduce_begin(0, 0)
    load_n.wait()
    back_spatial(0)
    if linked:
        reduce_second(0, 0)
        reduce_begin(0, 3)
    back_mix(0, (None, later(reduce_second, 0, 3), later(reduce_line, 1, 1)))
    back_norm_mid(0)
    if linked:
        reduce_first(0, 0)
    back_input_weights(0, half, (None, later(reduce_begin, 0, 2), later(reduce_second, 0, 2)), 2)
    if linked:
        reduce_begin(0, 1)
        reduce_first(0, 3)
        reduce_end(1)
        reduce_sent(1)
    back_input(0, (later(reduce_second, 0, 1), None, later(reduce_line, 0, 0), None))
    write_in = pltpu.make_async_copy(xf, grad_in, local_sem.at[0])
    write_in.start()
    if linked:
        vec_pair(0, links.twin).start()
        reduce_first(0, 2)
        reduce_first(0, 1)
        vec_add(0, links.twin)
        vec_pair(1, links.along_y).start()
        reduce_line(0, 3)
        vec_add(1, links.along_y)
        vec_pair(2, links.along_x).start()
        reduce_line(0, 2)
        vec_add(2, links.along_x)
        vec_line_begin()
        reduce_line(0, 1)
        reduce_sent(0)
        reduce_end(0)
        total = vec_line_end()
        for layer in range(LAYERS):
            mat_copy(layer).wait()
    else:
        total = vec_sum[...]
        for layer in range(LAYERS):
            copy = pltpu.make_async_copy(grads.at[layer], mat_out.at[layer], local_sem.at[1])
            copy.start()
            copy.wait()
    for layer in range(LAYERS):
        vec_out[layer : layer + 1, :] = total[:, layer * VEC : (layer + 1) * VEC]
    write_in.wait()


def per_device(wide, narrow, tokens, segment_ids, matrices, vectors, cotangent):
    axes = ("wide", "narrow")
    count, share = tokens.shape[0], matrices.shape[1]
    total = count * S
    linked = narrow == 4 and wide == 8 and share % 16 == 0
    if not linked:
        matrices = lax.all_gather(matrices, axes, axis=1, tiled=True)
    levels = wide // 2 if linked else 4
    anywhere = pl.BlockSpec(memory_space=pl.ANY)
    vmem = pl.BlockSpec(memory_space=pltpu.VMEM)
    mat_shape = (LAYERS, share, D) if linked else (LAYERS, ALL_ROWS, D)
    half, full = (total, HALF), (total, FF)
    dma = pltpu.SemaphoreType.DMA
    flags = dict(collective_id=0) if linked else {}
    results = pl.pallas_call(
        functools.partial(kernel, wide, narrow, linked),
        out_shape=(
            jax.ShapeDtypeStruct((total, D), F32),
            jax.ShapeDtypeStruct((total, D), F32),
            jax.ShapeDtypeStruct(mat_shape, F32 if linked else BF16),
            jax.ShapeDtypeStruct((LAYERS, VEC), F32),
            jax.ShapeDtypeStruct(half, BF16),
            jax.ShapeDtypeStruct(half, BF16),
            jax.ShapeDtypeStruct(half, BF16),
            jax.ShapeDtypeStruct(full, BF16),
        ),
        in_specs=[anywhere, vmem, anywhere, vmem, anywhere],
        out_specs=(anywhere, anywhere, anywhere, vmem) + (anywhere,) * 4,
        scratch_shapes=[
            pltpu.VMEM((LAYERS, ALL_ROWS, D), BF16),
            pltpu.VMEM((LAYERS, ALL_ROWS, D), BF16),
            pltpu.VMEM((ALL_ROWS if linked else 16, D), BF16),
            pltpu.VMEM(half, BF16),
            pltpu.VMEM(full, BF16),
            pltpu.VMEM(half, BF16),
            pltpu.VMEM(half, BF16),
            pltpu.VMEM((LAYERS, total, D), BF16),
            pltpu.VMEM((total, D), F32),
            pltpu.VMEM((total, D), BF16),
            pltpu.VMEM((count, S, S), BF16),
            pltpu.VMEM((count, S, S), BF16),
            pltpu.VMEM((LAYERS, total, 128), F32),
            pltpu.VMEM((LAYERS, total, 128), F32),
            pltpu.VMEM((total, 128), F32),
            pltpu.VMEM((total, 128), F32),
            pltpu.VMEM((total, HALF), F32),
            pltpu.VMEM((LAYERS, share if linked else 8, D), F32),
            pltpu.VMEM((count, S, 128), F32),
            pltpu.VMEM((S, 128), F32),
            pltpu.VMEM((S, 128), F32),
            pltpu.VMEM((LAYERS, VEC), F32),
            pltpu.VMEM((LAYERS, VEC), F32),
            pltpu.VMEM((1, LAYERS * VEC), F32),
            pltpu.VMEM((levels + 3, 1, LAYERS * VEC), F32),
            dma((7,)),
            pltpu.SemaphoreType.REGULAR,
            dma((LAYERS, levels, 7 + levels)),
            dma((LAYERS, levels, 8)),
            dma((LAYERS, levels, 8)),
            dma((LAYERS, levels, 8)),
            dma((levels + 3,)),
            dma((levels + 3,)),
        ],
        compiler_params=pltpu.CompilerParams(
            has_side_effects=True, vmem_limit_bytes=63 << 20, **flags
        ),
    )(
        tokens.reshape(total, D),
        segment_ids,
        matrices,
        vectors,
        cotangent.reshape(total, D),
    )
    out, grad_in, mat_grads, vec_grads = results[:4]
    if not linked:
        mat_grads = lax.psum_scatter(
            mat_grads.astype(F32), axes, scatter_dimension=1, tiled=True
        )
        vec_grads = lax.psum(vec_grads, axes)
    return (out.reshape(tokens.shape), grad_in.reshape(tokens.shape), mat_grads, vec_grads)


def solution(mesh):
    rows = P(("wide", "narrow"), None, None)
    spread = P(None, ("wide", "narrow"), None)
    return jax.shard_map(
        functools.partial(per_device, mesh.shape["wide"], mesh.shape["narrow"]),
        mesh=mesh,
        in_specs=(rows, P(("wide", "narrow"), None), spread, P(), rows),
        out_specs=(rows, rows, spread, P()),
        check_vma=False,
    )
```

```python
import functools

import jax
import jax.numpy as jnp
from jax import lax
from jax.experimental import pallas as pl
from jax.experimental.pallas import tpu as pltpu
from jax.sharding import PartitionSpec as P

D = 512
FF = 3072
HALF = FF // 2
S = 512
LAYERS = 2
VEC = D + HALF + S
ALL_ROWS = FF + HALF + S
EPSILON = 1e-05
BLOCK = 512
PART = 256
WIDTH = 256
MESH = pl.DeviceIdType.MESH
BF16 = jnp.bfloat16
F32 = jnp.float32
GELU_A = 0.7978845608028654
GELU_B = 0.044715


def dot(left, right, left_dim, right_dim):
    dims = (((left_dim,), (right_dim,)), ((), ()))
    return lax.dot_general(left, right, dims, preferred_element_type=F32)


def gelu_and_slope(z):
    squared = z * z
    share = 0.5 + 0.5 * jnp.tanh(z * (GELU_A + (GELU_A * GELU_B) * squared))
    value = z * share
    near, gate = value.astype(BF16), share.astype(BF16)
    rise = BF16(2.0 * GELU_A) + BF16(6.0 * GELU_A * GELU_B) * squared.astype(BF16)
    return value, gate + (near - near * gate) * rise


def lane_groups(values):
    total = values[:, :128]
    for at in range(128, values.shape[1], 128):
        total = total + values[:, at : at + 128]
    return total


def lanes(column, width):
    return jnp.concatenate([column] * (width // 128), axis=1)


class Links:
    def __init__(self, wide, narrow, share):
        self.share = share
        self.levels = wide // 2
        self.narrow = narrow
        self.w = lax.axis_index("wide")
        self.n = lax.axis_index("narrow")
        self.x = self.w % 2
        self.z = self.w // 2
        self.core = self.n % 2
        self.y = self.n // 2
        other_w = self.w + 1 - 2 * self.x
        other_n = self.n + 2 - 4 * self.y
        self.first = self.mix((other_w, self.n), (self.w, other_n))
        self.second = self.mix((self.w, other_n), (other_w, self.n))
        self.twin = (self.w, self.n + 1 - 2 * self.core)
        self.along_x = (other_w, self.n)
        self.along_y = (self.w, other_n)

    def mix(self, zero, one):
        return tuple((1 - self.core) * a + self.core * b for a, b in zip(zero, one))

    def line(self, z):
        return (2 * z + self.x, self.n)

    def partners(self):
        found = [self.twin, self.first, self.second]
        for step in range(1, self.levels):
            found.append(self.line((self.z + step) % self.levels))
        return found

    def rows(self, w, n):
        return pl.ds(pl.multiple_of((w * self.narrow + n) * self.share, 16), self.share)

    def shards(self, z):
        out = []
        for n, n_first, n_second, w_first, w_second in (
            (self.n, self.first[1], self.second[1], self.first[0], self.second[0]),
            (
                self.twin[1],
                self.twin[1] + (1 - self.core) * (2 - 4 * self.y),
                self.twin[1] + self.core * (2 - 4 * self.y),
                self.w + self.core * (1 - 2 * self.x),
                self.w + (1 - self.core) * (1 - 2 * self.x),
            ),
        ):
            cross = n + 2 - 4 * self.y
            out.append(self.rows(2 * z + self.x, n))
            out.append(self.rows(2 * z + w_first % 2, n_first))
            out.append(self.rows(2 * z + w_second % 2, n_second))
            out.append(self.rows(2 * z + 1 - self.x, cross))
        return out


def send(source, target, send_sem, recv_sem, device):
    return pltpu.make_async_remote_copy(
        src_ref=source,
        dst_ref=target,
        send_sem=send_sem,
        recv_sem=recv_sem,
        device_id=device,
        device_id_type=MESH,
    )


def kernel(wide, narrow, linked, tok, seg, mats, vec, cot, *refs):
    out, grad_in, mat_out, vec_out, park_u, park_s, park_n, park_g = refs[:8]
    (
        weights,
        grads,
        landing,
        u,
        gp,
        s,
        n,
        a,
        xf,
        xb,
        masked,
        masked_t,
        rstd_in,
        rstd_mid,
        acc1,
        acc2,
        vf,
        mat_stage,
        seg_t,
        bias_t,
        bias_sum,
        gains,
        inv_gains,
        vec_sum,
        vec_in,
        local_sem,
        credit,
        g_send,
        g_recv,
        r_send,
        r_recv,
        v_send,
        v_recv,
    ) = refs[8:]
    tokens = xf.shape[0]
    rows_here = tokens // S
    share = mats.shape[1]
    links = Links(wide, narrow, share) if linked else None
    levels = wide // 2 if linked else 4
    passed_on, started = ([], []), []

    load_tok = pltpu.make_async_copy(tok, xb, local_sem.at[0])
    load_tok.start()
    load_mats = []
    for layer in range(LAYERS):
        place = links.rows(links.w, links.n) if linked else pl.ds(0, ALL_ROWS)
        copy = pltpu.make_async_copy(
            mats.at[layer], weights.at[layer, place], local_sem.at[1 + layer]
        )
        copy.start()
        load_mats.append(copy)

    if linked:
        barrier = pltpu.get_barrier_semaphore()
        for device in links.partners():
            pl.semaphore_signal(barrier, inc=1, device_id=device, device_id_type=MESH)
        pl.semaphore_wait(barrier, len(links.partners()))

    if linked:
        sources, targets = [], []
        for step in range(levels):
            below = (links.z - step + 2 * levels) // (2 * levels)
            sources.append(below * (links.z - step) + (1 - below) * step)
        for step in range(1, levels):
            above = (levels - 1 - links.z - step + 2 * levels) // (2 * levels)
            upward = links.z + step
            downward = levels - 1 - step
            targets.append(links.line(above * upward + (1 - above) * downward))
        not_top = links.z < levels - 1
        shards_of = [links.shards(z) for z in sources]

    def gather_copy(layer, step, slot, send_slot, target_slot, device):
        rows = shards_of[step][slot]
        return send(
            weights.at[layer, rows],
            weights.at[layer, rows],
            g_send.at[layer, sources[step], send_slot],
            g_recv.at[layer, sources[step], target_slot],
            device,
        )

    def pass_on(layer, step, slot, send_slot, target_slot, device):
        again = functools.partial(gather_copy, layer, step, slot, send_slot, target_slot, device)
        again().start()
        passed_on[layer].append(again)

    def arrived(layer, step, slot):
        gather_copy(layer, step, slot, 0, slot, links.twin).wait_recv()

    def gather_depart(layer):
        load_mats[layer].wait()
        for at, device in enumerate(targets):
            pass_on(layer, 0, 0, 7 + at, 0, device)

    def gather_line(layer, step):
        if step:
            arrived(layer, step, 0)
        pass_on(layer, step, 0, 0, 1, links.first)
        pass_on(layer, step, 0, 1, 2, links.second)
        pass_on(layer, step, 0, 3, 4, links.twin)

    def gather_first(layer, step):
        arrived(layer, step, 1)
        pass_on(layer, step, 1, 2, 3, links.second)
        pass_on(layer, step, 1, 4, 5, links.twin)

    def gather_second(layer, step):
        for slot in (2, 3):
            arrived(layer, step, slot)
            pass_on(layer, step, slot, 3 + slot, 4 + slot, links.twin)

    def gather_twin(layer, step):
        for slot in range(4, 8):
            arrived(layer, step, slot)

    def gather_sent(layer):
        for again in passed_on[layer]:
            again().wait_send()

    if linked:
        shards_at = [links.shards(z) for z in range(levels)]
        own_shards = links.shards(links.z)

    def land(layer, index):
        rows = pl.ds(pl.multiple_of(index * share, 16), share)
        return weights.at[1, rows] if layer == 0 else landing.at[rows]

    def add_in(layer, rows, index):
        grads[layer, rows, :] = (
            grads[layer, rows, :].astype(F32) + land(layer, index)[...].astype(F32)
        ).astype(BF16)

    def reduce_copy(layer, z, rows, target, slot, device, recv_z=None):
        return send(
            grads.at[layer, rows],
            land(layer, target),
            r_send.at[layer, z, slot],
            r_recv.at[layer, z if recv_z is None else recv_z, slot],
            device,
        )

    def reduce_start(*where):
        reduce_copy(*where).start()
        started.append(where)

    def reduce_sent(layer):
        for where in started:
            if where[0] == layer:
                reduce_copy(*where).wait_send()

    def reduce_begin(layer, z):
        shards = shards_at[z]
        for slot in range(4):
            reduce_start(layer, z, shards[4 + slot], 4 * z + slot, slot, links.twin)

    def reduce_second(layer, z):
        shards = shards_at[z]
        for slot in (2, 3, 0, 1):
            reduce_copy(layer, z, shards[slot], 4 * z + slot, slot, links.twin).wait_recv()
            add_in(layer, shards[slot], 4 * z + slot)
            if slot >= 2:
                index = 4 * levels + 2 * z + slot - 2
                reduce_start(layer, z, shards[slot], index, 2 + slot, links.second)

    def reduce_first(layer, z):
        shards = shards_at[z]
        for slot in (1, 0):
            index = 4 * levels + 2 * z + slot
            reduce_copy(layer, z, shards[slot], index, 4 + slot, links.second).wait_recv()
            add_in(layer, shards[slot], index)
            if slot == 1:
                reduce_start(layer, z, shards[1], 6 * levels + z, 6, links.first)

    def line_copy(layer, z):
        return reduce_copy(
            layer, z, shards_at[z][0], 7 * levels + links.z, 7, links.line(z), links.z
        )

    def reduce_line(layer, z):
        shards = shards_at[z]
        index = 6 * levels + z
        reduce_copy(layer, z, shards[0], index, 6, links.first).wait_recv()
        add_in(layer, shards[0], index)

        @pl.when(links.z != z)
        def _():
            line_copy(layer, z).start()

    def mat_copy(layer):
        return pltpu.make_async_copy(mat_stage.at[layer], mat_out.at[layer], local_sem.at[1 + layer])

    def reduce_end(layer):
        shards = own_shards
        total = grads[layer, shards[0], :].astype(F32)
        for step in range(1, levels):
            z = (links.z + step) % levels
            reduce_copy(layer, z, shards[0], 7 * levels + z, 7, links.line(z)).wait_recv()
            total = total + land(layer, 7 * levels + z)[...].astype(F32)
        mat_stage[layer] = total
        mat_copy(layer).start()
        for z in range(levels):

            @pl.when(links.z != z)
            def _():
                line_copy(layer, z).wait_send()

    def vec_pair(index, device):
        return send(vec_sum, vec_in.at[levels + index], v_send.at[index], v_recv.at[index], device)

    def vec_add(index, device):
        vec_pair(index, device).wait()
        vec_sum[...] = vec_sum[...] + vec_in[levels + index]

    def vec_copy(step, z):
        return send(
            vec_sum,
            vec_in.at[z],
            v_send.at[2 + step],
            v_recv.at[3 + z],
            links.line((links.z + step) % levels),
        )

    def vec_line_begin():
        for step in range(1, levels):
            vec_copy(step, links.z).start()

    def vec_line_end():
        for step in range(1, levels):
            vec_copy(step, (links.z + step) % levels).wait_recv()
        for step in range(1, levels):
            vec_copy(step, links.z).wait_send()
        vec_in[pl.ds(links.z, 1)] = vec_sum[...][None]
        total = vec_in[0]
        for z in range(1, levels):
            total = total + vec_in[z]
        return total

    def prepare():
        gains[...] = vec[...].astype(F32)
        inv_gains[...] = 1.0 / gains[...]
        for r in range(rows_here):
            line = jnp.broadcast_to(seg[r : r + 1, :].astype(F32), (128, S))
            seg_t[r] = line.T
        acc1[...] = jnp.zeros_like(acc1)

    def same(r):
        return lanes(seg_t[r], S) == seg[r : r + 1, :].astype(F32)

    def row_chunk(i, size):
        return pl.ds(pl.multiple_of(i * size, size), size)

    def between(i, hooks):
        for at, hook in enumerate(hooks):
            if hook is not None:
                pl.when(i == at)(hook)

    def norm_in(layer):
        gain = gains[layer : layer + 1, :D]

        @pl.loop(0, tokens // 256)
        def _(i):
            found = []
            for part in range(2):
                rows = row_chunk(2 * i + part, 128)
                values = xb[rows, :].astype(F32) if layer == 0 else xf[rows, :]
                mean = jnp.sum(lane_groups(values), axis=1, keepdims=True) * (1.0 / D)
                found.append((rows, values - mean))
            for at, (rows, center) in enumerate(found):
                spread = jnp.sum(lane_groups(center * center), axis=1, keepdims=True) * (1.0 / D)
                found[at] = (rows, center, lax.rsqrt(spread + EPSILON))
            for rows, center, scale in found:
                a[layer, rows, :] = (center * scale * gain).astype(BF16)
                rstd_in[layer, rows, :] = jnp.broadcast_to(scale, (128, 128))

    def hidden(layer, z):
        per_level = ALL_ROWS // levels // WIDTH
        low, high, half = z * per_level, (z + 1) * per_level, HALF // WIDTH

        @pl.loop(jnp.minimum(low, half), jnp.minimum(high, half))
        def _(i):
            cols = row_chunk(i, WIDTH)
            for at in range(0, tokens, S):
                rows = pl.ds(at, S)
                value, slope = gelu_and_slope(dot(a[layer, rows, :], weights[layer, cols, :], 1, 1))
                u[rows, cols] = value.astype(BF16)
                gp[rows, cols] = slope

        @pl.loop(jnp.clip(low, half, 2 * half), jnp.clip(high, half, 2 * half))
        def _(i):
            cols_all = row_chunk(i, WIDTH)
            cols = row_chunk(i - half, WIDTH)
            for at in range(0, tokens, S):
                rows = pl.ds(at, S)
                z = dot(a[layer, rows, :], weights[layer, cols_all, :], 1, 1)
                value, slope = gelu_and_slope(z)
                vf[rows, cols] = value
                gp[rows, cols_all] = slope
                acc1[rows, :] += lane_groups(value)

    def norm_mid(layer):
        gain = gains[layer : layer + 1, D : D + HALF]
        for r in range(rows_here):
            rows = pl.ds(r * S, S)
            mean = jnp.sum(acc1[rows, :], axis=1, keepdims=True) * (1.0 / HALF)
            acc1[rows, :] = jnp.broadcast_to(mean, (S, 128))

        @pl.loop(0, tokens // 64)
        def _(i):
            rows = row_chunk(i, 64)
            center = vf[rows, :] - lanes(acc1[rows, :], HALF)
            acc2[rows, :] = lane_groups(center * center)

        for r in range(rows_here):
            rows = pl.ds(r * S, S)
            spread = jnp.sum(acc2[rows, :], axis=1, keepdims=True) * (1.0 / HALF)
            rstd_mid[layer, rows, :] = jnp.broadcast_to(lax.rsqrt(spread + EPSILON), (S, 128))

        @pl.loop(0, tokens // 64)
        def _(i):
            rows = row_chunk(i, 64)
            center = vf[rows, :] - lanes(acc1[rows, :], HALF)
            n[rows, :] = (center * lanes(rstd_mid[layer, rows, :], HALF) * gain).astype(BF16)

    def mask_weights(layer):
        spatial = weights[layer, FF + HALF :, :].astype(F32)
        spatial_t = spatial.T
        for r in range(rows_here):
            keep = same(r)
            masked[r] = jnp.where(keep, spatial, 0.0).astype(BF16)
            masked_t[r] = jnp.where(keep, spatial_t, 0.0).astype(BF16)
        line = jnp.broadcast_to(gains[layer : layer + 1, D + HALF :], (128, S))
        bias_t[...] = line.T

    def gated_rows(block, at, size):
        return pl.ds(pl.multiple_of(block * tokens + at, PART), size)

    def mix(layer, hooks=()):
        @pl.loop(0, HALF // BLOCK)
        def _(i):
            between(i, hooks)
            cols = row_chunk(i, BLOCK)
            for r in range(rows_here):
                for at in range(0, S, PART):
                    rows = pl.ds(r * S + at, PART)
                    mixed = dot(masked[r, at : at + PART, :], n[r * S : r * S + S, cols], 1, 0)
                    mixed = mixed + lanes(bias_t[at : at + PART, :], BLOCK)
                    s[rows, cols] = mixed.astype(BF16)
                    gated = (u[rows, cols].astype(F32) * mixed).astype(BF16)
                    grads[0, gated_rows(i, r * S + at, PART), :] = gated

    def project(layer, hooks=()):
        @pl.loop(0, tokens // S)
        def _(i):
            between(i, hooks)
            rows = row_chunk(i, S)
            values = xb[rows, :].astype(F32) if layer == 0 else xf[rows, :]
            for k in range(HALF // BLOCK):
                part = weights[layer, FF + k * BLOCK : FF + (k + 1) * BLOCK, :]
                values = values + dot(grads[0, gated_rows(k, i * S, S), :], part, 1, 0)
            if layer == LAYERS - 1:
                masked[i] = values.astype(BF16)
            else:
                xf[rows, :] = values

    def back_project(layer, hooks=(), weights_too=True):
        @pl.loop(0, HALF // BLOCK)
        def _(i):
            between(i, hooks)
            cols = row_chunk(i, BLOCK)
            w_rows = pl.ds(pl.multiple_of(FF + i * BLOCK, BLOCK), BLOCK)
            for at in range(0, tokens, PART):
                rows, here = pl.ds(at, PART), pl.ds(at % S, PART)
                dy = dot(xb[rows, :], weights[layer, w_rows, :], 1, 1).astype(BF16)
                gate, mixed = u[rows, cols], s[rows, cols]
                ds = dy * gate
                u[rows, cols] = gate * mixed
                s[rows, cols] = ds
                gp[rows, cols] = dy * mixed * gp[rows, cols]
                part = lane_groups(ds.astype(F32))
                if at < S:
                    part = part + jnp.where(i == 0, 0.0, bias_sum[here, :])
                else:
                    part = part + bias_sum[here, :]
                bias_sum[here, :] = part
            if weights_too:
                grads[layer, w_rows, :] = dot(u[:, cols], xb[...], 0, 0).astype(BF16)

    def back_output_weights(layer):
        @pl.loop(0, HALF // BLOCK)
        def _(i):
            w_rows = pl.ds(pl.multiple_of(FF + i * BLOCK, BLOCK), BLOCK)
            grads[layer, w_rows, :] = dot(u[:, row_chunk(i, BLOCK)], xb[...], 0, 0).astype(BF16)

    def back_input_weights(layer, low, hooks=(), turn=0):
        count = HALF // BLOCK

        @pl.loop(0, count)
        def _(i):
            between(i, hooks)
            cols = row_chunk(low + lax.rem(i + turn, count), BLOCK)
            grads[layer, cols, :] = dot(gp[:, cols], a[layer], 0, 0).astype(BF16)

    def back_spatial(layer):
        total = None
        for r in range(rows_here):
            rows = pl.ds(r * S, S)
            outer = jnp.where(same(r), dot(s[rows, :], n[rows, :], 1, 1), 0.0)
            total = outer if total is None else total + outer
        grads[layer, FF + HALF :, :] = total.astype(BF16)
        at = layer * VEC + D + HALF
        vec_sum[:, at : at + S] = jnp.sum(bias_sum[...].T, axis=0, keepdims=True)

    def back_mix(layer, hooks=()):
        @pl.loop(0, HALF // BLOCK)
        def _(i):
            between(i, hooks)
            cols = row_chunk(i, BLOCK)
            at_cols = pl.ds(pl.multiple_of(D + i * BLOCK, BLOCK), BLOCK)
            to = pl.ds(pl.multiple_of(layer * VEC + D + i * BLOCK, BLOCK), BLOCK)
            column = jnp.zeros((8, BLOCK), F32)
            for r in range(rows_here):
                for at in range(0, S, PART):
                    rows = pl.ds(r * S + at, PART)
                    dn = dot(masked_t[r, at : at + PART, :], s[r * S : r * S + S, cols], 1, 0)
                    e = dn * gains[layer : layer + 1, at_cols]
                    dn_n = dn * n[rows, cols].astype(F32)
                    vf[rows, cols] = e
                    part_e, part_ew = lane_groups(e), lane_groups(dn_n)
                    acc1[rows, :] = jnp.where(i == 0, part_e, acc1[rows, :] + part_e)
                    acc2[rows, :] = jnp.where(i == 0, part_ew, acc2[rows, :] + part_ew)
                    column = column + jnp.sum(dn_n.reshape(PART // 8, 8, BLOCK), axis=0)
            column = jnp.sum(column, axis=0, keepdims=True)
            vec_sum[:, to] = column * inv_gains[layer : layer + 1, at_cols]

    def back_norm_mid(layer):
        inverse = inv_gains[layer : layer + 1, D : D + HALF]
        for r in range(rows_here):
            rows = pl.ds(r * S, S)
            for acc in (acc1, acc2):
                mean = jnp.sum(acc[rows, :], axis=1, keepdims=True) * (1.0 / HALF)
                acc[rows, :] = jnp.broadcast_to(mean, (S, 128))

        @pl.loop(0, tokens // 64)
        def _(i):
            rows = row_chunk(i, 64)
            mean_e = lanes(acc1[rows, :], HALF)
            mean_ew = lanes(acc2[rows, :], HALF)
            dv = vf[rows, :] - mean_e - n[rows, :].astype(F32) * inverse * mean_ew
            dv = (dv * lanes(rstd_mid[layer, rows, :], HALF)).astype(BF16)
            gp[rows, HALF:] = dv * gp[rows, HALF:]

    def back_input(layer, hooks=()):
        gain = gains[layer : layer + 1, :D]
        inverse = inv_gains[layer : layer + 1, :D]
        at = layer * VEC
        vec_sum[:, at : at + D] = jnp.zeros((1, D), F32)

        @pl.loop(0, tokens // PART)
        def _(i):
            between(i, hooks)
            rows = row_chunk(i, PART)
            da = dot(gp[rows, :], weights[layer, :FF, :], 1, 0)
            normed = a[layer, rows, :].astype(F32)
            product = da * normed
            e = da * gain
            mean_e = jnp.sum(lane_groups(e), axis=1, keepdims=True) * (1.0 / D)
            mean_ew = jnp.sum(lane_groups(product), axis=1, keepdims=True) * (1.0 / D)
            dx = (e - mean_e - normed * inverse * mean_ew) * lanes(rstd_in[layer, rows, :], D)
            above = xb[rows, :].astype(F32) if layer == LAYERS - 1 else xf[rows, :]
            total = above + dx
            if layer:
                xf[rows, :] = total
                xb[rows, :] = total.astype(BF16)
            else:
                place = pl.ds(pl.multiple_of(lax.rem(i * PART, S), PART), PART)
                masked[i * PART // S, place, :] = total.astype(BF16)
            vec_sum[:, at : at + D] += jnp.sum(product, axis=0, keepdims=True) * inverse

    def later(act, *where):
        return (lambda: act(*where)) if linked else None

    def levels_in_turn(layer, after):
        last = levels - 2 + links.z // (levels - 1) if linked else levels - 1

        @pl.loop(0, levels)
        def _(step):
            if linked:
                between(step, [functools.partial(gather_twin, layer, k) for k in range(levels)])
                below = (links.z - step + 2 * levels) // (2 * levels)
                hidden(layer, below * (links.z - step) + (1 - below) * step)
                between(step, after)
            else:
                hidden(layer, step)
            pl.when(step == last)(lambda: norm_mid(layer))

    if linked:
        gather_depart(0)
        gather_line(0, 0)
        prepare()
        load_tok.wait()
        norm_in(0)
        gather_line(0, 1)
        gather_first(0, 0)
        gather_line(0, 2)
        gather_first(0, 1)
        gather_second(0, 0)
    else:
        prepare()
        for copy in load_mats:
            copy.wait()
        load_tok.wait()
        norm_in(0)

    def after_first():
        gather_first(0, 2)
        gather_second(0, 1)
        gather_line(0, 3)
        gather_depart(1)

    def after_second():
        gather_second(0, 2)
        gather_first(0, 3)
        gather_line(1, 0)

    def after_third():
        gather_second(0, 3)
        gather_line(1, 1)
        gather_first(1, 0)

    levels_in_turn(0, (after_first, after_second, after_third))
    keep_u = pltpu.make_async_copy(u, park_u, local_sem.at[3])
    keep_u.start()
    keep_g = pltpu.make_async_copy(gp, park_g, local_sem.at[4])
    keep_g.start()
    keep_n = pltpu.make_async_copy(n, park_n, local_sem.at[5])
    keep_n.start()
    mask_weights(0)
    mix(0, (later(gather_line, 1, 2), later(gather_first, 1, 1), None))
    keep_s = pltpu.make_async_copy(s, park_s, local_sem.at[6])
    keep_s.start()
    project(0, (None, later(gather_second, 1, 0)))
    load_cot = pltpu.make_async_copy(cot, xb, local_sem.at[0])
    load_cot.start()
    norm_in(1)
    acc1[...] = jnp.zeros_like(acc1)
    keep_u.wait()
    keep_g.wait()
    keep_n.wait()

    def after_first_again():
        gather_first(1, 2)
        gather_second(1, 1)
        gather_line(1, 3)

    def after_second_again():
        gather_first(1, 3)
        gather_second(1, 2)

    def after_third_again():
        gather_second(1, 3)

    if linked:
        gather_sent(0)
    levels_in_turn(1, (after_first_again, after_second_again, after_third_again))
    mask_weights(1)
    keep_s.wait()
    mix(1)
    load_cot.wait()

    back_project(1, weights_too=False)
    back_input_weights(1, 0)
    if linked:
        reduce_begin(1, 0)
    back_output_weights(1)
    load_u = pltpu.make_async_copy(park_u, u, local_sem.at[3])
    load_u.start()
    if linked:
        reduce_second(1, 0)
    back_spatial(1)
    if linked:
        reduce_begin(1, 3)
    project(1)
    write_out = pltpu.make_async_copy(masked, out, local_sem.at[1])
    write_out.start()
    if linked:
        reduce_second(1, 3)
    back_mix(1)
    load_s = pltpu.make_async_copy(park_s, s, local_sem.at[6])
    load_s.start()
    back_norm_mid(1)
    load_n = pltpu.make_async_copy(park_n, n, local_sem.at[5])
    load_n.start()
    if linked:
        reduce_first(1, 0)
    half = HALF // BLOCK
    back_input_weights(1, half, (None, later(reduce_begin, 1, 2), later(reduce_second, 1, 2)), 2)
    if linked:
        reduce_begin(1, 1)
        reduce_first(1, 3)
    write_out.wait()
    back_input(1, (later(reduce_second, 1, 1), None, later(reduce_line, 1, 0), None))
    load_g = pltpu.make_async_copy(park_g, gp, local_sem.at[4])
    load_g.start()
    if linked:
        gather_sent(1)
        for device in links.partners():
            pl.semaphore_signal(credit, inc=1, device_id=device, device_id_type=MESH)
        reduce_first(1, 2)

    mask_weights(0)
    load_u.wait()
    load_s.wait()
    load_g.wait()
    back_project(0, (None, later(reduce_line, 1, 3), None))
    back_input_weights(0, 0, (later(reduce_first, 1, 1), None, later(reduce_line, 1, 2)))
    if linked:
        pl.semaphore_wait(credit, len(links.partners()))
        reduce_begin(0, 0)
    load_n.wait()
    back_spatial(0)
    if linked:
        reduce_second(0, 0)
        reduce_begin(0, 3)
    back_mix(0, (None, later(reduce_second, 0, 3), later(reduce_line, 1, 1)))
    back_norm_mid(0)
    if linked:
        reduce_first(0, 0)
    back_input_weights(0, half, (None, later(reduce_begin, 0, 2), later(reduce_second, 0, 2)), 2)
    if linked:
        reduce_begin(0, 1)
        reduce_first(0, 3)
        reduce_end(1)
        reduce_sent(1)
    back_input(0, (later(reduce_second, 0, 1), None, later(reduce_line, 0, 0), None))
    write_in = pltpu.make_async_copy(masked, grad_in, local_sem.at[0])
    write_in.start()
    if linked:
        vec_pair(0, links.twin).start()
        reduce_first(0, 2)
        reduce_first(0, 1)
        vec_add(0, links.twin)
        vec_pair(1, links.along_y).start()
        reduce_line(0, 3)
        vec_add(1, links.along_y)
        vec_pair(2, links.along_x).start()
        reduce_line(0, 2)
        vec_add(2, links.along_x)
        vec_line_begin()
        reduce_line(0, 1)
        reduce_sent(0)
        reduce_end(0)
        total = vec_line_end()
        for layer in range(LAYERS):
            mat_copy(layer).wait()
    else:
        total = vec_sum[...]
        for layer in range(LAYERS):
            copy = pltpu.make_async_copy(grads.at[layer], mat_out.at[layer], local_sem.at[1])
            copy.start()
            copy.wait()
    for layer in range(LAYERS):
        vec_out[layer : layer + 1, :] = total[:, layer * VEC : (layer + 1) * VEC]
    write_in.wait()


def per_device(wide, narrow, tokens, segment_ids, matrices, vectors, cotangent):
    axes = ("wide", "narrow")
    count, share = tokens.shape[0], matrices.shape[1]
    total = count * S
    linked = narrow == 4 and wide == 8 and share % 16 == 0
    if not linked:
        matrices = lax.all_gather(matrices, axes, axis=1, tiled=True)
    levels = wide // 2 if linked else 4
    anywhere = pl.BlockSpec(memory_space=pl.ANY)
    vmem = pl.BlockSpec(memory_space=pltpu.VMEM)
    mat_shape = (LAYERS, share, D) if linked else (LAYERS, ALL_ROWS, D)
    half, full = (total, HALF), (total, FF)
    dma = pltpu.SemaphoreType.DMA
    flags = dict(collective_id=0) if linked else {}
    results = pl.pallas_call(
        functools.partial(kernel, wide, narrow, linked),
        out_shape=(
            jax.ShapeDtypeStruct((count, S, D), BF16),
            jax.ShapeDtypeStruct((count, S, D), BF16),
            jax.ShapeDtypeStruct(mat_shape, F32 if linked else BF16),
            jax.ShapeDtypeStruct((LAYERS, VEC), F32),
            jax.ShapeDtypeStruct(half, BF16),
            jax.ShapeDtypeStruct(half, BF16),
            jax.ShapeDtypeStruct(half, BF16),
            jax.ShapeDtypeStruct(full, BF16),
        ),
        in_specs=[anywhere, vmem, anywhere, vmem, anywhere],
        out_specs=(anywhere, anywhere, anywhere, vmem) + (anywhere,) * 4,
        scratch_shapes=[
            pltpu.VMEM((LAYERS, ALL_ROWS, D), BF16),
            pltpu.VMEM((LAYERS, ALL_ROWS, D), BF16),
            pltpu.VMEM((ALL_ROWS if linked else 16, D), BF16),
            pltpu.VMEM(half, BF16),
            pltpu.VMEM(full, BF16),
            pltpu.VMEM(half, BF16),
            pltpu.VMEM(half, BF16),
            pltpu.VMEM((LAYERS, total, D), BF16),
            pltpu.VMEM((total, D), F32),
            pltpu.VMEM((total, D), BF16),
            pltpu.VMEM((count, S, S), BF16),
            pltpu.VMEM((count, S, S), BF16),
            pltpu.VMEM((LAYERS, total, 128), F32),
            pltpu.VMEM((LAYERS, total, 128), F32),
            pltpu.VMEM((total, 128), F32),
            pltpu.VMEM((total, 128), F32),
            pltpu.VMEM((total, HALF), F32),
            pltpu.VMEM((LAYERS, share if linked else 8, D), F32),
            pltpu.VMEM((count, S, 128), F32),
            pltpu.VMEM((S, 128), F32),
            pltpu.VMEM((S, 128), F32),
            pltpu.VMEM((LAYERS, VEC), F32),
            pltpu.VMEM((LAYERS, VEC), F32),
            pltpu.VMEM((1, LAYERS * VEC), F32),
            pltpu.VMEM((levels + 3, 1, LAYERS * VEC), F32),
            dma((7,)),
            pltpu.SemaphoreType.REGULAR,
            dma((LAYERS, levels, 7 + levels)),
            dma((LAYERS, levels, 8)),
            dma((LAYERS, levels, 8)),
            dma((LAYERS, levels, 8)),
            dma((levels + 3,)),
            dma((levels + 3,)),
        ],
        compiler_params=pltpu.CompilerParams(
            has_side_effects=True, vmem_limit_bytes=63 << 20, **flags
        ),
    )(
        tokens.reshape(total, D),
        segment_ids,
        matrices,
        vectors,
        cotangent.reshape(total, D),
    )
    out, grad_in, mat_grads, vec_grads = results[:4]
    if not linked:
        mat_grads = lax.psum_scatter(
            mat_grads.astype(F32), axes, scatter_dimension=1, tiled=True
        )
        vec_grads = lax.psum(vec_grads, axes)
    return (out.astype(F32), grad_in.astype(F32), mat_grads, vec_grads)


def solution(mesh):
    rows = P(("wide", "narrow"), None, None)
    spread = P(None, ("wide", "narrow"), None)
    return jax.shard_map(
        functools.partial(per_device, mesh.shape["wide"], mesh.shape["narrow"]),
        mesh=mesh,
        in_specs=(rows, P(("wide", "narrow"), None), spread, P(), rows),
        out_specs=(rows, rows, spread, P()),
        check_vma=False,
    )
```
